32 devices in a mesh: dp: 8 (over z, core), tensor: 2 (over x), group: 2 (over y).
Axes of the slice: x: 2, y: 2, z: 4, core: 2. Of those that a mesh axis runs over, the one named last changes fastest.
Arguments:
- tokens: bfloat16 [2048, 5120], P(('dp', 'group')), may hold values from -6 to 6
- cotangent: bfloat16 [2048, 1024], P(('dp', 'group'), 'tensor'), may hold values from -0.13183594 to 0.13183594
- counts: int32 [16], replicated, may hold values from 32 to 128, as said below
- old_offsets: int32 [4, 9], replicated, may hold values from 0 to 1310720, as said below
- old_master: float32 [4, 8, 204800], P(('tensor', 'group'), 'dp'), may hold values from -0.078125 to 0.078125
- old_moment: float32 [4, 8, 204800], P(('tensor', 'group'), 'dp'), may hold values from -3 to 3
- old_variance: float32 [4, 8, 204800], P(('tensor', 'group'), 'dp'), may hold values from 0.001 to 1
- old_grad: float32 [4, 8, 204800], P(('tensor', 'group'), 'dp'), may hold values from -6 to 6
Outputs:
- activated: bfloat16 [2048, 1024], P(('dp', 'group'), 'tensor')
- new_master: float32 [5120, 1024], P(('dp', 'group'), 'tensor')
- new_moment: float32 [5120, 1024], P(('dp', 'group'), 'tensor')
- new_variance: float32 [5120, 1024], P(('dp', 'group'), 'tensor')
The draws below stay inside these ranges and needn't reach their ends.
Inputs may be any that keep to these rules, and one draw needn't show every extreme that they name: `counts`: each new data rank has between 32 and 128 live tokens, which fill its first slots; in every draw some rank has exactly 128. `old_offsets`: each row starts at 0 and ends at 1310720; entry p lies within 20480 of p * 163840; in every row some entry p with 0 < p < 8 equals p * 163840 + 20480.
All inputs are finite; a program needn't handle non-finite values.
Results may differ from the reference program's by a relative error of at most 0.0051.
Values may be sent and summed in bfloat16 or wider, within the bound.
No kernel may reach another device: no remote copies, remote signals or barrier semaphores. Data moves between devices by JAX's collectives and lax.ppermute only.
A program may use at most 64 MiB of HBM per device.

```python
import math
import jax
import jax.numpy as jnp

D = 5120
KV = 1024
TOK = 128
DATA = 16
TOKENS = 2048
OLD_RANKS = 8
OLD_SLABS = 4
OLD_COLS = 256
SHARD = 163840
SLACK = 20480
WINDOW = 204800


def draw_counts(key, part):
    drawn = jax.random.randint(jax.random.fold_in(key, 11), (DATA,), TOK // 4, TOK + 1)
    chosen = jax.random.randint(jax.random.fold_in(key, 12), (), 0, DATA)
    return jnp.where(jnp.arange(DATA) == chosen, TOK, drawn).astype(jnp.int32)


def draw_old_offsets(key, part):
    offset_shift = jax.random.randint(jax.random.fold_in(key, 21), (OLD_SLABS, OLD_RANKS + 1), -SLACK, SLACK + 1)
    chosen = jax.random.randint(jax.random.fold_in(key, 22), (OLD_SLABS, 1), 1, OLD_RANKS)
    column_index = jnp.arange(OLD_RANKS + 1)[None, :]
    offset_shift = jnp.where(column_index == chosen, SLACK, offset_shift)
    offset_shift = jnp.where((column_index == 0) | (column_index == OLD_RANKS), 0, offset_shift)
    return (column_index * SHARD + offset_shift).astype(jnp.int32)


def shard_levels(key, extent, cuts, least, top_value):
    def one(axis_at, shards_of):
        draws = jax.random.uniform(jax.random.fold_in(jax.random.fold_in(key, 6), axis_at), (shards_of,), jnp.float32, least / len(cuts), top_value / len(cuts))
        return jnp.repeat(jnp.exp(draws), extent[axis_at] // shards_of).reshape((-1,) + (1,) * (len(extent) - axis_at - 1))

    factor_of = one(*cuts[0])
    for cut in cuts[1:]:
        factor_of = factor_of * one(*cut)
    return factor_of


def noise(own_key, shape, deviation, most, shards=(), kind=jnp.bfloat16):
    values = jax.random.normal(own_key, shape, jnp.float32) * deviation
    if len(shards) > 0:
        values = shard_levels(own_key, shape, shards, -0.22, 0.18) * values
    return jnp.clip(values, min=-most, max=most).astype(kind)


def setup_inputs(seed: int = 0) -> dict:
    streams_of = jax.random.split(jax.random.key(seed), 9)
    tokens = noise(streams_of[0], (TOKENS, D), 1.0, 6.0, ((0, 16),))
    cotangent = noise(streams_of[1], (TOKENS, KV), (TOKENS ** -0.5), 0.13183594, ((0, 16), (1, 2)))
    counts = draw_counts(jax.random.fold_in(streams_of[8], 71), 0)
    old_offsets = draw_old_offsets(jax.random.fold_in(streams_of[8], 71), 0)
    old_master = noise(streams_of[4], (OLD_SLABS, OLD_RANKS, WINDOW), D ** -0.5, 0.078125, ((0, 4), (1, 8)), jnp.float32)
    old_moment = noise(streams_of[5], (OLD_SLABS, OLD_RANKS, WINDOW), 0.5, 3.0, ((0, 4), (1, 8)), jnp.float32)
    old_variance = jnp.clip(jnp.exp(math.log(1.0) - 6.9077552 * jax.random.uniform(streams_of[6], (OLD_SLABS, OLD_RANKS, WINDOW), jnp.float32) ** shard_levels(streams_of[6], (OLD_SLABS, OLD_RANKS, WINDOW), ((0, 4), (1, 8)), -0.2, 0.2)), 0.001, 1.0)
    old_grad = noise(streams_of[7], (OLD_SLABS, OLD_RANKS, WINDOW), 1.0, 6.0, ((0, 4), (1, 8)), jnp.float32)
    return {"tokens": tokens, "cotangent": cotangent, "counts": counts, "old_offsets": old_offsets, "old_master": old_master, "old_moment": old_moment, "old_variance": old_variance, "old_grad": old_grad}


beta_one = 0.9
beta_two = 0.95
epsilon = 1e-08
learn_rate = 0.001
weight_decay = 0.1
first_step = 3.0
second_step = 4.0

def adam_update(master, moment, variance, gradient, step_count):
    moment = beta_one * moment + (1.0 - beta_one) * gradient
    variance = beta_two * variance + (1.0 - beta_two) * gradient * gradient
    fix_one = 1.0 - beta_one ** step_count
    fix_two = 1.0 - beta_two ** step_count
    update = moment / fix_one / (jnp.sqrt(variance / fix_two) + epsilon) + weight_decay * master
    return (master - learn_rate * update, moment, variance)

def rebuild(windows, old_offsets):
    slab_count, old_ranks, window = windows.shape[1:]
    position = jnp.arange(old_ranks, dtype=jnp.int32)[:, None] * SHARD - SLACK + jnp.arange(window, dtype=jnp.int32)[None, :]
    low_edge = old_offsets[:, :-1][:, :, None]
    high_edge = old_offsets[:, 1:][:, :, None]
    is_live = (position[None] >= low_edge) & (position[None] < high_edge)
    masked = jnp.where(is_live[None], windows, jnp.float32(0.0))
    target = jnp.clip(position, 0, SHARD * old_ranks - 1).astype(jnp.int32)
    flat_state = jnp.zeros((3, slab_count, SHARD * old_ranks), jnp.float32)
    flat_state = flat_state.at[:, :, target].add(masked)
    whole_state = flat_state.reshape(3, slab_count, D, OLD_COLS).transpose(0, 2, 1, 3)
    return whole_state.reshape(3, D, KV)

def reference(tokens, cotangent, counts, old_offsets, old_master, old_moment, old_variance, old_grad):
    master, moment, variance = adam_update(old_master, old_moment, old_variance, old_grad, first_step)
    states = rebuild(jnp.stack([master, moment, variance]), old_offsets)
    weights = states[0].astype(jnp.bfloat16)
    preact = jnp.dot(tokens, weights, preferred_element_type=jnp.float32)
    activated = jax.nn.silu(preact).astype(jnp.bfloat16)
    sigmoid_z = jax.nn.sigmoid(preact)
    derivative = sigmoid_z * (1.0 + preact * (1.0 - sigmoid_z))
    row_ids = jnp.arange(TOKENS, dtype=jnp.int32)
    is_live = row_ids % TOK < counts[row_ids // TOK]
    delta = jnp.where(is_live[:, None], cotangent.astype(jnp.float32) * derivative, jnp.float32(0.0)).astype(jnp.bfloat16)
    gradient = jnp.dot(tokens.T, delta, preferred_element_type=jnp.float32)
    new_master, new_moment, new_variance = adam_update(states[0], states[1], states[2], gradient, second_step)
    return (activated, new_master, new_moment, new_variance)
```

```python
import jax
import jax.numpy as jnp
from jax import lax
from jax.sharding import PartitionSpec as P

beta_one = 0.9
beta_two = 0.95
epsilon = 1e-08
learn_rate = 0.001
weight_decay = 0.1
first_step = 3.0
second_step = 4.0

LANES = 128
CORES = 2


def swap(value, axis, bits):
    pairs = [(source, source ^ bits) for source in range(lax.axis_size(axis))]
    return lax.ppermute(value, axis, pairs)


def swap_border(value):
    pairs = []
    for right in range(CORES, lax.axis_size("dp"), CORES):
        pairs += [(right - 1, right), (right, right - 1)]
    return lax.ppermute(value, "dp", pairs)


def adam_update(master, moment, variance, gradient, step_count):
    moment = beta_one * moment + (1.0 - beta_one) * gradient
    variance = beta_two * variance + (1.0 - beta_two) * gradient * gradient
    fix_one = 1.0 - beta_one**step_count
    fix_two = 1.0 - beta_two**step_count
    update = moment / fix_one / (jnp.sqrt(variance / fix_two) + epsilon) + weight_decay * master
    return (master - learn_rate * update, moment, variance)


def local(tokens, cotangent, counts, old_offsets, old_master, old_moment, old_variance, old_grad):
    f32, bf16 = jnp.float32, jnp.bfloat16
    ranks = lax.axis_size("dp")
    chips = ranks // CORES
    groups = lax.axis_size("group")
    rank = lax.axis_index("dp")
    chip, core = rank // CORES, rank % CORES
    group = lax.axis_index("group")
    slab = lax.axis_index("tensor") * groups + group
    slots, width = tokens.shape
    cols = cotangent.shape[1]
    old_cols = cols // groups
    depth = width // chips

    def token_block(of_chip):
        return lax.dynamic_slice(tokens, (0, of_chip * depth), (slots, depth))

    blocks = [token_block(chip)]
    for step in range(1, chips):
        blocks.append(swap(token_block(chip ^ step), "dp", step * CORES))

    windows = jnp.stack([old_master[0, 0], old_moment[0, 0], old_variance[0, 0], old_grad[0, 0]])
    length = windows.shape[1]
    margin = length // 10
    shard = length - 2 * margin
    windows = windows.reshape(4, 10, margin // LANES, LANES)
    head, tail = windows[:, 0], windows[:, 9]
    first = core == 0
    inner = swap(jnp.where(first, tail, head), "dp", 1)
    outer = swap_border(jnp.where(first, head, tail))
    from_left = jnp.where(first, outer, inner)
    from_right = jnp.where(first, inner, outer)
    bounds = lax.dynamic_slice(old_offsets, (slab, rank), (1, 2))[0] - rank * shard
    place = lax.broadcasted_iota(jnp.int32, head.shape[1:], 0) * LANES
    place = place + lax.broadcasted_iota(jnp.int32, head.shape[1:], 1)
    left = jnp.where(place < bounds[0], from_left, windows[:, 1])
    right = jnp.where(place + (shard - margin) >= bounds[1], from_right, windows[:, 8])
    nominal = jnp.concatenate([left[:, None], windows[:, 2:8], right[:, None]], axis=1)
    states = jnp.stack(adam_update(*nominal, first_step))
    piece = shard // old_cols
    states = states.reshape(3, piece, old_cols)
    tile = piece // groups

    own = states[0].astype(bf16)
    other = swap(own, "group", 1)
    low = group == 0
    wide = jnp.concatenate([jnp.where(low, own, other), jnp.where(low, other, own)], axis=1)
    mate = swap(wide, "dp", 1)
    weights = jnp.concatenate(
        [jnp.where(first, wide, mate), jnp.where(first, mate, wide)], axis=0
    )

    outgoing = lax.dynamic_slice_in_dim(states, (1 - group) * tile, tile, 1)
    staying = lax.dynamic_slice_in_dim(states, group * tile, tile, 1)
    incoming = swap(outgoing, "group", 1)
    states = jnp.concatenate(
        [jnp.where(low, staying, incoming), jnp.where(low, incoming, staying)], axis=2
    )

    total = jnp.dot(blocks[0], weights, preferred_element_type=f32)
    for step in range(1, chips):
        part = jnp.dot(blocks[step], weights, preferred_element_type=f32).astype(bf16)
        total = total + swap(part, "dp", step * CORES).astype(f32)
    preact = total
    activated = jax.nn.silu(preact).astype(bf16)
    sigmoid = jax.nn.sigmoid(preact)
    derivative = sigmoid * (1.0 + preact * (1.0 - sigmoid))
    live = jnp.arange(slots, dtype=jnp.int32) < counts[rank * groups + group]
    delta = jnp.where(live[:, None], cotangent.astype(f32) * derivative, 0.0).astype(bf16)

    contract = (((0,), (0,)), ((), ()))
    deltas = [delta] + [swap(delta, "dp", step * CORES) for step in range(1, chips)]
    gradient = lax.dot_general(
        jnp.concatenate(blocks), jnp.concatenate(deltas), contract, preferred_element_type=f32
    )
    gradient = gradient.reshape(CORES, groups, tile, cols)
    keep = lax.dynamic_index_in_dim(gradient, core, 0, keepdims=False)
    send = lax.dynamic_index_in_dim(gradient, 1 - core, 0, keepdims=False)
    gradient = keep + swap(send.astype(bf16), "dp", 1).astype(f32)
    keep = lax.dynamic_index_in_dim(gradient, group, 0, keepdims=False)
    send = lax.dynamic_index_in_dim(gradient, 1 - group, 0, keepdims=False)
    gradient = keep + swap(send.astype(bf16), "group", 1).astype(f32)

    new_master, new_moment, new_variance = adam_update(*states, gradient, second_step)
    return (activated, new_master, new_moment, new_variance)


def solution(mesh):
    rows = P(("dp", "group"), "tensor")
    window = P(("tensor", "group"), "dp", None)
    return jax.shard_map(
        local,
        mesh=mesh,
        in_specs=(P(("dp", "group"), None), rows, P(), P(), window, window, window, window),
        out_specs=(rows, rows, rows, rows),
        check_vma=False,
    )
```

```python
import functools

import jax
import jax.numpy as jnp
from jax import lax
from jax.experimental import pallas as pl
from jax.experimental.pallas import tpu as pltpu
from jax.sharding import PartitionSpec as P

beta_one = 0.9
beta_two = 0.95
epsilon = 1e-08
learn_rate = 0.001
weight_decay = 0.1
first_step = 3.0
second_step = 4.0

LANES = 128
CORES = 2
f32, bf16 = jnp.float32, jnp.bfloat16
VMEM = 16 * 2**20
LONG = 10**11


def swap(value, axis, bits):
    pairs = [(source, source ^ bits) for source in range(lax.axis_size(axis))]
    return lax.ppermute(value, axis, pairs)


def swap_border(value):
    pairs = []
    for right in range(CORES, lax.axis_size("dp"), CORES):
        pairs += [(right - 1, right), (right, right - 1)]
    return lax.ppermute(value, "dp", pairs)


def adam_update(master, moment, variance, gradient, step_count):
    moment = beta_one * moment + (1.0 - beta_one) * gradient
    variance = beta_two * variance + (1.0 - beta_two) * gradient * gradient
    fix_one = 1.0 / (1.0 - beta_one**step_count)
    fix_two = 1.0 / (1.0 - beta_two**step_count)
    update = moment * fix_one / (jnp.sqrt(variance * fix_two) + epsilon) + weight_decay * master
    return (master - learn_rate * update, moment, variance)


def call(kernel, shapes, *args, scalars=0, flops=0):
    whole = pl.BlockSpec(memory_space=pltpu.VMEM)
    small = pl.BlockSpec(memory_space=pltpu.SMEM)
    touched = sum(a.size * a.dtype.itemsize for a in args)
    return pl.pallas_call(
        kernel,
        out_shape=shapes,
        in_specs=[small] * scalars + [whole] * (len(args) - scalars),
        out_specs=jax.tree.map(lambda _: whole, shapes),
        compiler_params=pltpu.CompilerParams(vmem_limit_bytes=VMEM),
        cost_estimate=pl.CostEstimate(flops=flops, bytes_accessed=touched, transcendentals=0),
    )(*args)


def shape(dims, dtype):
    return jax.ShapeDtypeStruct(dims, dtype)


def first_kernel(moves, *refs):
    windows, refs = refs[:4], refs[4:]
    tokens, refs = (refs[0], refs[1:]) if moves else (None, refs)
    weights, leaving, staying, end_states = refs[:4]
    blocks, (held, sems, *block_sems) = refs[4 : 4 + moves], refs[4 + moves :]
    group, tensor, rank = (lax.axis_index(a) for a in ("group", "tensor", "dp"))
    tensors = lax.axis_size("tensor")
    chip, core = rank // CORES, rank % CORES
    rows, cols = weights.shape[1:]
    count = weights.shape[0] - 2
    half, per = count // 2, cols // LANES
    runs = [(0, 1), (count + 1, 1), ((1 - group) * half + 1, half), (group * half + 1, half)]
    copies = [
        [
            pltpu.make_async_copy(
                windows[i].at[pl.ds(start, size)], held.at[i, pl.ds(start, size)], sems.at[j, i]
            )
            for i in range(4)
        ]
        for j, (start, size) in enumerate(runs)
    ]
    moved = []
    for step, out in enumerate(blocks):
        share, depth = out.shape[0] // (tensors if step == 0 else 1), out.shape[1] // CORES
        for j in range(out.shape[0] // share):
            row = pl.multiple_of((tensor ^ j) * share, share)
            for i in range(CORES):
                col = pl.multiple_of(((chip ^ step) * CORES + (core ^ i)) * depth, depth)
                moved.append(
                    pltpu.make_async_copy(
                        tokens.at[pl.ds(row, share), pl.ds(col, depth)],
                        out.at[pl.ds(j * share, share), pl.ds(i * depth, depth)],
                        block_sems[0].at[step, j, i],
                    )
                )
    for copy in [c for run in copies for c in run] + moved:
        copy.start()

    def update(block, h):
        picks = pl.ds(h, rows, stride=per) if per > 1 else pl.ds(0, rows)
        return adam_update(*[held[i, block, picks, :] for i in range(4)], first_step)

    for j, (start, size) in enumerate(runs):
        for copy in copies[j]:
            copy.wait()
        for k in range(size):
            for h in range(per):
                at = slice(h * LANES, (h + 1) * LANES)
                values = update(start + k, h)
                weights[start + k, :, at] = values[0].astype(bf16)
                if j < 2:
                    for i in range(3):
                        end_states[j, i, :, at] = values[i]
                else:
                    for i in range(3):
                        (leaving, staying)[j - 2][i, k, :, at] = values[i]
    for copy in moved:
        copy.wait()


def first(windows, tokens, old_cols, chips, tensors):
    count, rows = windows[0].shape[0] - 2, windows[0].shape[1]
    short = rows * LANES // old_cols
    slots, depth = tokens.shape[0], tokens.shape[1] // chips
    share = slots // tensors
    aligned = depth % (CORES * LANES) == 0 and share % 16 == 0
    moves = chips if aligned else 0
    blocks = [shape((slots if i == 0 else share, depth), bf16) for i in range(moves)]
    tile = shape((3, count // 2, short, old_cols), f32)
    outs = [
        shape((count + 2, short, old_cols), bf16),
        tile,
        tile,
        shape((2, 3, short, old_cols), f32),
        *blocks,
    ]
    operands = [*windows, tokens] if moves else windows
    scratch = [pltpu.VMEM((4, count + 2, rows, LANES), f32), pltpu.SemaphoreType.DMA((4, 4))]
    if moves:
        scratch.append(pltpu.SemaphoreType.DMA((chips, tensors, CORES)))
    out = pl.pallas_call(
        functools.partial(first_kernel, moves),
        out_shape=outs,
        in_specs=[pl.BlockSpec(memory_space=pl.ANY)] * len(operands),
        out_specs=[pl.BlockSpec(memory_space=pltpu.VMEM)] * len(outs),
        scratch_shapes=scratch,
        cost_estimate=pl.CostEstimate(flops=0, bytes_accessed=10**7, transcendentals=0),
    )(*operands)
    return out[:4], out[4:]


def live_bounds(offsets, span, rank, other):
    slab = lax.axis_index("tensor") * lax.axis_size("group") + (lax.axis_index("group") ^ other)
    start = rank * span
    return offsets[slab, rank] - start, offsets[slab, rank + 1] - start


def place_of(rows, cols, first):
    place = lax.broadcasted_iota(jnp.int32, (rows, cols), 0) * cols
    return first + place + lax.broadcasted_iota(jnp.int32, (rows, cols), 1)


def patch_weights_kernel(offsets, mine, other, inner, outer, out):
    rows, cols = mine.shape[1:]
    count = mine.shape[0] - 2
    span = count * rows * cols
    is_first = lax.axis_index("dp") % CORES == 0
    for i, piece in enumerate((mine, other)):
        at = slice(i * cols, (i + 1) * cols)
        low, high = live_bounds(offsets, span, lax.axis_index("dp"), i)
        near, far = inner[:, at].astype(f32), outer[:, at].astype(f32)
        before = place_of(rows, cols, 0) < low
        after = place_of(rows, cols, span - rows * cols) >= high
        begin, end = piece[1].astype(f32), piece[count].astype(f32)
        out[0, :, at] = jnp.where(before, jnp.where(is_first, far, near), begin).astype(bf16)
        out[1 : count - 1, :, at] = piece[2:count]
        out[count - 1, :, at] = jnp.where(after, jnp.where(is_first, near, far), end).astype(bf16)


def patch_states_kernel(offsets, leaving, staying, inner, outer, out_leaving, out_staying):
    _, half, rows, cols = leaving.shape
    span = 2 * half * rows * cols
    low, high = live_bounds(offsets, span, lax.axis_index("dp"), 0)
    first = lax.axis_index("dp") % CORES == 0
    group = lax.axis_index("group")
    for tile, states, out in ((1 - group, leaving, out_leaving), (group, staying, out_staying)):
        before = place_of(rows, cols, tile * (span // 2)) < low
        after = place_of(rows, cols, tile * (span // 2) + (half - 1) * rows * cols) >= high
        for i in range(3):
            left = jnp.where(first, outer[i], inner[i])
            right = jnp.where(first, inner[i], outer[i])
            out[i, 0] = jnp.where(before, left, states[i, 0])
            out[i, 1 : half - 1] = states[i, 1 : half - 1]
            out[i, half - 1] = jnp.where(after, right, states[i, half - 1])


def part_kernel(pieces, *refs):
    mine, mate, out = refs[pieces:]
    rows = jnp.concatenate([r[...] for r in refs[:pieces]], axis=0)
    depth = mine.shape[0]
    value = jnp.dot(rows[:, :depth], mine[...], preferred_element_type=f32)
    value = value + jnp.dot(rows[:, depth:], mate[...], preferred_element_type=f32)
    out[...] = value.astype(out.dtype)


def part(pieces, weights, dtype):
    rows = sum(p.shape[0] for p in pieces)
    cols = weights[0].shape[1]
    return call(
        functools.partial(part_kernel, len(pieces)),
        shape((rows, cols), dtype),
        *pieces,
        *weights,
        flops=2 * rows * pieces[0].shape[1] * cols,
    )


def own_order(rows, cols):
    tensors, groups = lax.axis_size("tensor"), lax.axis_size("group")
    share, wide = rows // tensors, cols // groups
    for j in range(tensors):
        row = pl.multiple_of((lax.axis_index("tensor") ^ j) * share, share)
        for i in range(groups):
            col = pl.multiple_of((lax.axis_index("group") ^ i) * wide, wide)
            here = (slice(j * share, (j + 1) * share), slice(i * wide, (i + 1) * wide))
            yield here, (pl.ds(row, share), pl.ds(col, wide)), row


def live_kernel(counts, _, cotangent, out):
    live = counts[lax.axis_index("dp") * lax.axis_size("group") + lax.axis_index("group")]
    for here, there, first_row in own_order(*cotangent.shape):
        value = cotangent[there].astype(f32)
        row = first_row + lax.broadcasted_iota(jnp.int32, value.shape, 0)
        out[here] = jnp.where(row < live, value, 0.0).astype(bf16)


def delta_kernel(*refs):
    own, (cotangent, activated, delta) = refs[0], refs[-3:]
    preact = own[...]
    for r in refs[1:-3]:
        preact = preact + r[...].astype(f32)
    sigmoid = 1.0 / (1.0 + jnp.exp(-preact))
    activated[...] = (preact * sigmoid).astype(bf16)
    derivative = sigmoid * (1.0 + preact * (1.0 - sigmoid))
    delta[...] = (cotangent[...].astype(f32) * derivative).astype(bf16)


def natural_kernel(value, out):
    for here, there, _ in own_order(*value.shape):
        out[there] = value[here]


def gradient_kernel(tokens, *refs):
    deltas, out = refs[:-1], refs[-1]
    delta = jnp.concatenate([r[...] for r in deltas], axis=0)
    value = lax.dot_general(
        tokens[...], delta, (((0,), (0,)), ((), ())), preferred_element_type=f32
    ).astype(out.dtype)
    tile = out.shape[1]
    for i in range(out.shape[0]):
        out[i] = value[i * tile : (i + 1) * tile]


def core_sum_kernel(mine, received, keep, send):
    group = lax.axis_index("group")
    cols = keep.shape[1] // 2
    keep[...] = mine[group] + received[group].astype(f32)
    value = (mine[1 - group] + received[1 - group].astype(f32)).astype(bf16)
    send[:, :cols] = value[:, cols:]
    send[:, cols:] = value[:, :cols]


def second_adam_kernel(staying, incoming, keep, back, master, moment, variance):
    cols = staying.shape[2]
    group = lax.axis_index("group")
    for i, states in enumerate((staying, incoming)):
        here = slice(i * cols, (i + 1) * cols)
        there = pl.ds(pl.multiple_of((group ^ i) * cols, cols), cols)
        gradient = keep[:, here] + back[:, here].astype(f32)
        result = adam_update(states[0], states[1], states[2], gradient, second_step)
        for ref, value in zip((master, moment, variance), result, strict=True):
            ref[:, there] = value


def local(tokens, cotangent, counts, old_offsets, old_master, old_moment, old_variance, old_grad):
    ranks = lax.axis_size("dp")
    chips = ranks // CORES
    groups = lax.axis_size("group")
    tensors = lax.axis_size("tensor")
    rank = lax.axis_index("dp")
    chip, core = rank // CORES, rank % CORES
    tensor = lax.axis_index("tensor")
    slots, width = tokens.shape
    cols = cotangent.shape[1]
    old_cols = cols // groups
    depth = width // chips
    half = depth // CORES
    share = slots // tensors

    length = old_master.shape[2]
    margin = length // 10
    windows = [
        w.reshape(10, margin // LANES, LANES)
        for w in (old_master, old_moment, old_variance, old_grad)
    ]
    (window, leaving, staying, end_states), blocks = first(
        windows, tokens, old_cols, chips, tensors
    )

    def token_block(of_chip, of_tensor):
        return jnp.concatenate(
            [
                lax.dynamic_slice(
                    tokens, (of_tensor * share, of_chip * depth + (core ^ i) * half), (share, half)
                )
                for i in range(CORES)
            ],
            axis=1,
        )

    blocks = blocks or [
        jnp.concatenate([token_block(chip, tensor ^ j) for j in range(tensors)]),
        *[token_block(chip ^ step, tensor) for step in range(1, chips)],
    ]
    turned = call(
        live_kernel, shape((slots, cols), bf16), counts, window, cotangent, scalars=1, flops=LONG
    )
    arrived = [swap(b, "dp", step * CORES) for step, b in enumerate(blocks) if step]
    arrived = [lax.optimization_barrier((a, turned))[0] for a in arrived]
    blocks = [[blocks[0]]] + [
        [a] + [swap(a, "tensor", j) for j in range(1, tensors)] for a in arrived
    ]

    other = swap(window, "group", 1)
    ends = [jnp.concatenate([window[i], other[i]], axis=1) for i in (0, -1)]
    inner = swap(jnp.where(core == 0, ends[1], ends[0]), "dp", 1)
    outer = swap_border(jnp.where(core == 0, ends[0], ends[1]))
    count, rows = window.shape[0] - 2, window.shape[1]
    mine = call(
        patch_weights_kernel,
        shape((count, rows, cols), bf16),
        old_offsets,
        window,
        other,
        inner,
        outer,
        scalars=1,
    )
    mine = mine.reshape(half, cols)
    weights = [mine, swap(mine, "dp", 1)]

    parts = [part(blocks[step], weights, bf16) for step in range(1, chips)]
    back = [swap(p, "dp", step * CORES) for step, p in enumerate(parts, 1)]

    total = part(blocks[0], weights, f32)

    end_states, arrived[-1] = lax.optimization_barrier((end_states, arrived[-1]))
    mate_end = swap(jnp.where(core == 0, end_states[1], end_states[0]), "dp", 1)
    next_end = swap_border(jnp.where(core == 0, end_states[0], end_states[1]))
    leaving, *parts = lax.optimization_barrier((leaving, *parts))
    leaving, staying = call(
        patch_states_kernel,
        [shape(leaving.shape, f32)] * 2,
        old_offsets,
        leaving,
        staying,
        mate_end,
        next_end,
        scalars=1,
    )
    tile = half // groups
    staying = staying.reshape(3, tile, old_cols)
    incoming = swap(leaving.reshape(3, tile, old_cols), "group", 1)
    activated, delta = call(
        delta_kernel, [shape((slots, cols), bf16)] * 2, total, *back, turned
    )
    activated = call(natural_kernel, shape((slots, cols), bf16), activated)
    deltas = [delta] + [swap(delta, "dp", step * CORES) for step in range(1, chips)]

    deltas[-1], incoming = lax.optimization_barrier((deltas[-1], incoming))

    gathered = jnp.concatenate([p for b in blocks for p in b])
    flops = 2 * half * cols * chips * slots
    rows = (groups, tile, cols)
    to_mate = call(gradient_kernel, shape(rows, bf16), gathered[:, half:], *deltas, flops=flops)
    mine = call(gradient_kernel, shape(rows, f32), gathered[:, :half], *deltas, flops=flops)
    keep, send = call(
        core_sum_kernel,
        [shape((tile, cols), f32), shape((tile, cols), bf16)],
        mine,
        swap(to_mate, "dp", 1),
    )
    new = call(
        second_adam_kernel,
        [shape((tile, cols), f32)] * 3,
        staying,
        incoming,
        keep,
        swap(send, "group", 1),
    )
    return (activated, *new)


def solution(mesh):
    rows = P(("dp", "group"), "tensor")
    window = P(("tensor", "group"), "dp", None)
    return jax.shard_map(
        local,
        mesh=mesh,
        in_specs=(P(("dp", "group"), None), rows, P(), P(), window, window, window, window),
        out_specs=(rows, rows, rows, rows),
        check_vma=False,
    )
```

```python
import functools

import jax
import jax.numpy as jnp
from jax import lax
from jax.experimental import pallas as pl
from jax.experimental.pallas import tpu as pltpu
from jax.sharding import PartitionSpec as P

beta_one = 0.9
beta_two = 0.95
epsilon = 1e-08
learn_rate = 0.001
weight_decay = 0.1
first_step = 3.0
second_step = 4.0

LANES = 128
CORES = 2
f32, bf16 = jnp.float32, jnp.bfloat16
VMEM = 16 * 2**20
DIRECT = 2
LONG = 10**11


def swap(value, axis, bits):
    pairs = [(source, source ^ bits) for source in range(lax.axis_size(axis))]
    return lax.ppermute(value, axis, pairs)


def swap_border(value):
    pairs = []
    for right in range(CORES, lax.axis_size("dp"), CORES):
        pairs += [(right - 1, right), (right, right - 1)]
    return lax.ppermute(value, "dp", pairs)


def adam_update(master, moment, variance, gradient, step_count):
    moment = beta_one * moment + (1.0 - beta_one) * gradient
    variance = beta_two * variance + (1.0 - beta_two) * gradient * gradient
    fix_one = 1.0 / (1.0 - beta_one**step_count)
    fix_two = 1.0 / (1.0 - beta_two**step_count)
    update = moment * fix_one / (jnp.sqrt(variance * fix_two) + epsilon) + weight_decay * master
    return (master - learn_rate * update, moment, variance)


def call(kernel, shapes, *args, scalars=0, flops=0, after=()):
    whole = pl.BlockSpec(memory_space=pltpu.VMEM)
    small = pl.BlockSpec(memory_space=pltpu.SMEM)
    touched = sum(a.size * a.dtype.itemsize for a in args)
    end = len(args)

    def body(*refs):
        kernel(*refs[:end], *refs[end + len(after) :])

    return pl.pallas_call(
        body,
        out_shape=shapes,
        in_specs=[small] * scalars
        + [whole] * (end - scalars)
        + [pl.BlockSpec(memory_space=pl.ANY)] * len(after),
        out_specs=jax.tree.map(lambda _: whole, shapes),
        compiler_params=pltpu.CompilerParams(vmem_limit_bytes=VMEM),
        cost_estimate=pl.CostEstimate(flops=flops, bytes_accessed=touched, transcendentals=0),
    )(*args, *after)


def shape(dims, dtype):
    return jax.ShapeDtypeStruct(dims, dtype)


def blocks_kernel(steps, skip, tokens, *refs):
    outs, sems = refs[skip:-1], refs[-1]
    rank, tensor = lax.axis_index("dp"), lax.axis_index("tensor")
    chip, core = rank // CORES, rank % CORES
    share = tokens.shape[0] // lax.axis_size("tensor")
    copies = []
    for step, out in zip(steps, outs, strict=True):
        depth = out.shape[1] // CORES
        for j in range(out.shape[0] // share):
            row = pl.multiple_of((tensor ^ j) * share, share)
            for i in range(CORES):
                col = pl.multiple_of(((chip ^ step) * CORES + (core ^ i)) * depth, depth)
                copies.append(
                    pltpu.make_async_copy(
                        tokens.at[pl.ds(row, share), pl.ds(col, depth)],
                        out.at[pl.ds(j * share, share), pl.ds(i * depth, depth)],
                        sems.at[len(copies)],
                    )
                )
    for copy in copies:
        copy.start()
    for copy in copies:
        copy.wait()


def token_blocks(tokens, steps, share, depth, after):
    slots = tokens.shape[0]
    outs = [shape((slots if step < DIRECT else share, depth), bf16) for step in steps]
    copies = sum(CORES * (out.shape[0] // share) for out in outs)
    return pl.pallas_call(
        functools.partial(blocks_kernel, steps, len(after)),
        out_shape=outs,
        in_specs=[pl.BlockSpec(memory_space=pl.ANY)] * (1 + len(after)),
        out_specs=[pl.BlockSpec(memory_space=pltpu.VMEM)] * len(outs),
        scratch_shapes=[pltpu.SemaphoreType.DMA((copies,))],
        compiler_params=pltpu.CompilerParams(vmem_limit_bytes=VMEM),
        cost_estimate=pl.CostEstimate(flops=0, bytes_accessed=10**6, transcendentals=0),
    )(tokens, *after)


def first_adam_kernel(*refs):
    windows, (weights, leaving, staying, ends) = refs[:4], refs[4:]
    group = lax.axis_index("group")
    _, half, rows, cols = staying.shape
    per = cols // LANES
    runs = [(ends.at[0], 0, 1), (ends.at[1], 2 * half + 1, 1)]
    runs += [(leaving, (1 - group) * half + 1, half), (staying, group * half + 1, half)]
    for out, start, size in runs:
        for k in range(size):
            for h in range(per):
                at = slice(h * LANES, (h + 1) * LANES)
                picks = pl.ds(h, rows, stride=per) if per > 1 else pl.ds(0, rows)
                values = adam_update(*[w[start + k, picks, :] for w in windows], first_step)
                weights[start + k, :, at] = values[0].astype(bf16)
                for i in range(3):
                    out[i, k, :, at] = values[i].astype(out.dtype)


def first_adam(windows, old_cols, after):
    count, rows = windows[0].shape[0] - 2, windows[0].shape[1]
    short = rows * LANES // old_cols
    tile = shape((3, count // 2, short, old_cols), f32)
    ends = shape((2, 3, 1, short, old_cols), bf16)
    weights = shape((count + 2, short, old_cols), bf16)
    return call(first_adam_kernel, [weights, tile, tile, ends], *windows, after=after)


def live_bounds(offsets, span, rank, other):
    slab = lax.axis_index("tensor") * lax.axis_size("group") + (lax.axis_index("group") ^ other)
    start = rank * span
    return offsets[slab, rank] - start, offsets[slab, rank + 1] - start


def place_of(rows, cols, first):
    place = lax.broadcasted_iota(jnp.int32, (rows, cols), 0) * cols
    return first + place + lax.broadcasted_iota(jnp.int32, (rows, cols), 1)


def patch_weights_kernel(offsets, own, other, mate_own, mate_other, outer, mate_outer, mine, mate):
    rows, cols = own.shape[1:]
    count = own.shape[0] - 2
    span = count * rows * cols
    rank = lax.axis_index("dp")
    first = rank % CORES == 0
    for i, (here, there) in enumerate(((own, mate_own), (other, mate_other))):
        at = slice(i * cols, (i + 1) * cols)
        for out, window, near, far, swapped in (
            (mine, here, there, outer, 0),
            (mate, there, here, mate_outer, 1),
        ):
            low, high = live_bounds(offsets, span, rank ^ swapped, i)
            left_far = first if swapped == 0 else jnp.logical_not(first)
            before = place_of(rows, cols, 0) < low
            after = place_of(rows, cols, span - rows * cols) >= high
            far_end = far[i].astype(f32)
            left = jnp.where(left_far, far_end, near[count + 1].astype(f32))
            right = jnp.where(left_far, near[0].astype(f32), far_end)
            out[0, :, at] = jnp.where(before, left, window[1].astype(f32)).astype(bf16)
            out[1 : count - 1, :, at] = window[2:count]
            out[count - 1, :, at] = jnp.where(after, right, window[count].astype(f32)).astype(bf16)


def patch_states_kernel(offsets, leaving, staying, inner, outer, out_leaving, out_staying):
    _, half, rows, cols = leaving.shape
    span = 2 * half * rows * cols
    low, high = live_bounds(offsets, span, lax.axis_index("dp"), 0)
    first = lax.axis_index("dp") % CORES == 0
    group = lax.axis_index("group")
    for tile, states, out in ((1 - group, leaving, out_leaving), (group, staying, out_staying)):
        before = place_of(rows, cols, tile * (span // 2)) < low
        after = place_of(rows, cols, tile * (span // 2) + (half - 1) * rows * cols) >= high
        for i in range(3):
            near, far = inner[i].astype(f32), outer[i].astype(f32)
            left, right = jnp.where(first, far, near), jnp.where(first, near, far)
            out[i, 0] = jnp.where(before, left, states[i, 0]).astype(out.dtype)
            out[i, 1 : half - 1] = states[i, 1 : half - 1].astype(out.dtype)
            out[i, half - 1] = jnp.where(after, right, states[i, half - 1]).astype(out.dtype)


def part_kernel(pieces, *refs):
    mine, mate, out = refs[pieces:]
    rows = jnp.concatenate([r[...] for r in refs[:pieces]], axis=0)
    depth = mine.shape[0]
    value = jnp.dot(rows[:, :depth], mine[...], preferred_element_type=f32)
    value = value + jnp.dot(rows[:, depth:], mate[...], preferred_element_type=f32)
    out[...] = value.astype(out.dtype)


def part(pieces, weights, dtype, flops=0, after=()):
    rows = sum(p.shape[0] for p in pieces)
    cols = weights[0].shape[1]
    return call(
        functools.partial(part_kernel, len(pieces)),
        shape((rows, cols), dtype),
        *pieces,
        *weights,
        flops=flops or 2 * rows * pieces[0].shape[1] * cols,
        after=after,
    )


def own_order(rows, cols):
    tensors, groups = lax.axis_size("tensor"), lax.axis_size("group")
    share, wide = rows // tensors, cols // groups
    for j in range(tensors):
        row = pl.multiple_of((lax.axis_index("tensor") ^ j) * share, share)
        for i in range(groups):
            col = pl.multiple_of((lax.axis_index("group") ^ i) * wide, wide)
            here = (slice(j * share, (j + 1) * share), slice(i * wide, (i + 1) * wide))
            yield here, (pl.ds(row, share), pl.ds(col, wide)), row


def live_kernel(counts, cotangent, out):
    live = counts[lax.axis_index("dp") * lax.axis_size("group") + lax.axis_index("group")]
    for here, there, first_row in own_order(*cotangent.shape):
        value = cotangent[there].astype(f32)
        row = first_row + lax.broadcasted_iota(jnp.int32, value.shape, 0)
        out[here] = jnp.where(row < live, value, 0.0).astype(bf16)


def delta_kernel(*refs):
    own, (cotangent, activated, delta) = refs[0], refs[-3:]
    preact = own[...]
    for r in refs[1:-3]:
        preact = preact + r[...].astype(f32)
    sigmoid = 1.0 / (1.0 + jnp.exp(-preact))
    activated[...] = (preact * sigmoid).astype(bf16)
    derivative = sigmoid * (1.0 + preact * (1.0 - sigmoid))
    delta[...] = (cotangent[...].astype(f32) * derivative).astype(bf16)


def natural_kernel(value, out):
    for here, there, _ in own_order(*value.shape):
        out[there] = value[here]


def place_kernel(value, out):
    out[...] = value[...]


def zero_kernel(out):
    out[...] = jnp.zeros(out.shape, out.dtype)


def gather_kernel(*refs):
    start = 0
    for r in refs[:-1]:
        refs[-1][start : start + r.shape[0]] = r[...]
        start += r.shape[0]


def gradient_kernel(second, tokens, *refs):
    deltas, out = refs[:-1], refs[-1]
    depth = tokens.shape[1] // CORES
    value = lax.dot_general(
        tokens[:, depth * second : depth * (second + 1)],
        jnp.concatenate([r[...] for r in deltas], axis=0),
        (((0,), (0,)), ((), ())),
        preferred_element_type=f32,
    ).astype(out.dtype)
    tile = out.shape[1]
    for i in range(out.shape[0]):
        out[i] = value[i * tile : (i + 1) * tile]


def core_sum_kernel(mine, received, keep, send):
    group = lax.axis_index("group")
    cols = keep.shape[1] // 2
    keep[...] = mine[group] + received[group].astype(f32)
    value = (mine[1 - group] + received[1 - group].astype(f32)).astype(bf16)
    send[:, :cols] = value[:, cols:]
    send[:, cols:] = value[:, :cols]


def second_adam_kernel(staying, incoming, keep, back, master, moment, variance):
    _, half, rows, cols = staying.shape
    group = lax.axis_index("group")
    for k in range(half):
        for i, states in enumerate((staying, incoming)):
            here = (slice(k * rows, (k + 1) * rows), slice(i * cols, (i + 1) * cols))
            there = pl.ds(pl.multiple_of((group ^ i) * cols, cols), cols)
            gradient = keep[here] + back[here].astype(f32)
            values = [states[j, k].astype(f32) for j in range(3)]
            result = adam_update(*values, gradient, second_step)
            for ref, value in zip((master, moment, variance), result, strict=True):
                ref[k * rows : (k + 1) * rows, there] = value


def local(tokens, cotangent, counts, old_offsets, old_master, old_moment, old_variance, old_grad):
    ranks = lax.axis_size("dp")
    chips = ranks // CORES
    groups = lax.axis_size("group")
    tensors = lax.axis_size("tensor")
    rank = lax.axis_index("dp")
    chip, core = rank // CORES, rank % CORES
    tensor = lax.axis_index("tensor")
    slots, width = tokens.shape
    cols = cotangent.shape[1]
    old_cols = cols // groups
    depth = width // chips
    half = depth // CORES
    share = slots // tensors

    length = old_master.shape[2]
    margin = length // 10
    windows = [
        w.reshape(10, margin // LANES, LANES)
        for w in (old_master, old_moment, old_variance, old_grad)
    ]
    ahead = call(zero_kernel, shape((8, LANES), f32), flops=LONG)
    window, leaving, staying, ends = first_adam(windows, old_cols, [ahead])

    def token_block(of_chip, of_tensor):
        return jnp.concatenate(
            [
                lax.dynamic_slice(
                    tokens, (of_tensor * share, of_chip * depth + (core ^ i) * half), (share, half)
                )
                for i in range(CORES)
            ],
            axis=1,
        )

    def blocks_of(steps, after):
        if half % LANES == 0 and share % 16 == 0:
            return token_blocks(tokens, steps, share, depth, after)
        return [
            jnp.concatenate(
                [
                    token_block(chip ^ step, tensor ^ j)
                    for j in range(tensors if step < DIRECT else 1)
                ]
            )
            for step in steps
        ]

    leaving_blocks = blocks_of(range(1, chips), [])

    cleared = call(place_kernel, shape(window.shape[1:], bf16), window[0], flops=LONG)
    other = swap(window, "group", 1)
    arrived = [swap(b, "dp", step * CORES) for step, b in enumerate(leaving_blocks, 1)]
    arrived = [lax.optimization_barrier((a, cleared))[0] for a in arrived]

    ends = jnp.concatenate([ends[:, :, 0], jnp.stack([other[0], other[-1]])[:, None]], axis=1)
    inner = swap(jnp.where(core == 0, ends[1], ends[0]), "dp", 1)
    outer = swap_border(jnp.where(core == 0, ends[0], ends[1]))

    turned = call(
        live_kernel, shape((slots, cols), bf16), counts, cotangent, scalars=1, after=[other]
    )
    blocks = [[b] for b in [*blocks_of(range(1), [other]), *arrived]]
    for block in blocks[DIRECT:]:
        block += [swap(block[0], "tensor", j) for j in range(1, tensors)]

    far, _ = lax.optimization_barrier((jnp.stack([outer[0], outer[3]]), blocks[DIRECT]))
    leaving, far = lax.optimization_barrier((leaving, far))
    leaving, staying = call(
        patch_states_kernel,
        [shape(leaving.shape, bf16), shape(leaving.shape, f32)],
        old_offsets,
        leaving,
        staying,
        inner,
        outer,
        scalars=1,
    )
    incoming = swap(leaving, "group", 1)

    count, rows = window.shape[0] - 2, window.shape[1]
    mates = [swap(w, "dp", 1) for w in (window, other, far)]
    window, *_ = lax.optimization_barrier((window, leaving, *blocks[-1]))
    weights = call(
        patch_weights_kernel,
        [shape((count, rows, cols), bf16)] * 2,
        old_offsets,
        window,
        other,
        *mates[:2],
        far,
        mates[2],
        scalars=1,
    )
    weights = [w.reshape(half, cols) for w in weights]

    steps = range(chips - 1, 0, -1)
    parts = []
    for step in steps:
        parts.append(part(blocks[step], weights, bf16, after=parts[-1:]))
    back = [swap(p, "dp", step * CORES) for step, p in zip(steps, parts, strict=True)]

    own_block, *_ = lax.optimization_barrier((blocks[0][0], *parts))
    total = part([own_block], weights, f32, LONG)
    total, incoming = lax.optimization_barrier((total, incoming))
    activated, delta = call(
        delta_kernel, [shape((slots, cols), bf16)] * 2, total, *back, turned
    )

    deltas = [delta] + [swap(delta, "dp", step * CORES) for step in steps]

    flat = [p for step in (0, *steps) for p in blocks[step]]
    flat[0], _ = lax.optimization_barrier((flat[0], delta))
    gathered = call(gather_kernel, shape((chips * slots, depth), bf16), *flat, flops=LONG)
    flops = 2 * half * cols * chips * slots
    tile = half // groups
    to_mate, mine = (
        call(
            functools.partial(gradient_kernel, second),
            shape((groups, tile, cols), dtype),
            gathered,
            *deltas,
            flops=flops,
        )
        for second, dtype in ((1, bf16), (0, f32))
    )
    keep, send = call(
        core_sum_kernel,
        [shape((tile, cols), f32), shape((tile, cols), bf16)],
        mine,
        swap(to_mate, "dp", 1),
    )
    new = call(
        second_adam_kernel,
        [shape((tile, cols), f32)] * 3,
        staying,
        incoming,
        keep,
        swap(send, "group", 1),
    )
    activated = call(natural_kernel, shape((slots, cols), bf16), activated)
    return (activated, *new)


def solution(mesh):
    rows = P(("dp", "group"), "tensor")
    window = P(("tensor", "group"), "dp", None)
    return jax.shard_map(
        local,
        mesh=mesh,
        in_specs=(P(("dp", "group"), None), rows, P(), P(), window, window, window, window),
        out_specs=(rows, rows, rows, rows),
        check_vma=False,
    )
```

```python
import functools

import jax
import jax.numpy as jnp
from jax import lax
from jax.experimental import pallas as pl
from jax.experimental.pallas import tpu as pltpu
from jax.sharding import PartitionSpec as P

beta_one = 0.9
beta_two = 0.95
epsilon = 1e-08
learn_rate = 0.001
weight_decay = 0.1
first_step = 3.0
second_step = 4.0

LANES = 128
CORES = 2
f32, bf16 = jnp.float32, jnp.bfloat16
VMEM = 16 * 2**20
DIRECT = 2
LONG = 10**11


def swap(value, axis, bits):
    pairs = [(source, source ^ bits) for source in range(lax.axis_size(axis))]
    return lax.ppermute(value, axis, pairs)


def swap_border(value):
    pairs = []
    for right in range(CORES, lax.axis_size("dp"), CORES):
        pairs += [(right - 1, right), (right, right - 1)]
    return lax.ppermute(value, "dp", pairs)


def adam_update(master, moment, variance, gradient, step_count):
    moment = beta_one * moment + (1.0 - beta_one) * gradient
    variance = beta_two * variance + (1.0 - beta_two) * gradient * gradient
    fix_one = 1.0 / (1.0 - beta_one**step_count)
    fix_two = 1.0 / (1.0 - beta_two**step_count)
    update = moment * fix_one / (jnp.sqrt(variance * fix_two) + epsilon) + weight_decay * master
    return (master - learn_rate * update, moment, variance)


def call(kernel, shapes, *args, scalars=0, flops=0, after=()):
    whole = pl.BlockSpec(memory_space=pltpu.VMEM)
    small = pl.BlockSpec(memory_space=pltpu.SMEM)
    touched = sum(a.size * a.dtype.itemsize for a in args)
    end = len(args)

    def body(*refs):
        kernel(*refs[:end], *refs[end + len(after) :])

    return pl.pallas_call(
        body,
        out_shape=shapes,
        in_specs=[small] * scalars
        + [whole] * (end - scalars)
        + [pl.BlockSpec(memory_space=pl.ANY)] * len(after),
        out_specs=jax.tree.map(lambda _: whole, shapes),
        compiler_params=pltpu.CompilerParams(vmem_limit_bytes=VMEM),
        cost_estimate=pl.CostEstimate(flops=flops, bytes_accessed=touched, transcendentals=0),
    )(*args, *after)


def shape(dims, dtype):
    return jax.ShapeDtypeStruct(dims, dtype)


def blocks_kernel(steps, skip, tokens, *refs):
    outs, sems = refs[skip:-1], refs[-1]
    rank, tensor = lax.axis_index("dp"), lax.axis_index("tensor")
    chip, core = rank // CORES, rank % CORES
    share = tokens.shape[0] // lax.axis_size("tensor")
    copies = []
    for step, out in zip(steps, outs, strict=True):
        depth = out.shape[1] // CORES
        for j in range(out.shape[0] // share):
            row = pl.multiple_of((tensor ^ j) * share, share)
            for i in range(CORES):
                col = pl.multiple_of(((chip ^ step) * CORES + (core ^ i)) * depth, depth)
                copies.append(
                    pltpu.make_async_copy(
                        tokens.at[pl.ds(row, share), pl.ds(col, depth)],
                        out.at[pl.ds(j * share, share), pl.ds(i * depth, depth)],
                        sems.at[len(copies)],
                    )
                )
    for copy in copies:
        copy.start()
    for copy in copies:
        copy.wait()


def token_blocks(tokens, steps, share, depth, after):
    slots = tokens.shape[0]
    outs = [shape((slots if step < DIRECT else share, depth), bf16) for step in steps]
    copies = sum(CORES * (out.shape[0] // share) for out in outs)
    return pl.pallas_call(
        functools.partial(blocks_kernel, steps, len(after)),
        out_shape=outs,
        in_specs=[pl.BlockSpec(memory_space=pl.ANY)] * (1 + len(after)),
        out_specs=[pl.BlockSpec(memory_space=pltpu.VMEM)] * len(outs),
        scratch_shapes=[pltpu.SemaphoreType.DMA((copies,))],
        compiler_params=pltpu.CompilerParams(vmem_limit_bytes=VMEM),
        cost_estimate=pl.CostEstimate(flops=0, bytes_accessed=10**6, transcendentals=0),
    )(tokens, *after)


def updated(windows, block, h, rows, per):
    picks = pl.ds(h, rows, stride=per) if per > 1 else pl.ds(0, rows)
    return adam_update(*[w[block, picks, :] for w in windows], first_step)


def first_weights_kernel(*refs):
    windows, out = refs[:4], refs[4]
    blocks, rows, cols = out.shape
    per = cols // LANES
    for k in range(blocks):
        for h in range(per):
            value = updated(windows, k, h, rows, per)[0]
            out[k, :, h * LANES : (h + 1) * LANES] = value.astype(bf16)


def first_states_kernel(*refs):
    windows, (leaving, staying, ends) = refs[:4], refs[4:]
    group = lax.axis_index("group")
    _, half, rows, cols = staying.shape
    per = cols // LANES
    runs = [(ends.at[0], 0, 1), (ends.at[1], 2 * half + 1, 1)]
    runs += [(leaving, (1 - group) * half + 1, half), (staying, group * half + 1, half)]
    for out, start, size in runs:
        for k in range(size):
            for h in range(per):
                values = updated(windows, start + k, h, rows, per)
                for i in range(3):
                    out[i, k, :, h * LANES : (h + 1) * LANES] = values[i].astype(out.dtype)


def live_bounds(offsets, span, rank, other):
    slab = lax.axis_index("tensor") * lax.axis_size("group") + (lax.axis_index("group") ^ other)
    start = rank * span
    return offsets[slab, rank] - start, offsets[slab, rank + 1] - start


def place_of(rows, cols, first):
    place = lax.broadcasted_iota(jnp.int32, (rows, cols), 0) * cols
    return first + place + lax.broadcasted_iota(jnp.int32, (rows, cols), 1)


def patch_weights_kernel(offsets, own, other, mate_own, mate_other, outer, mate_outer, mine, mate):
    rows, cols = own.shape[1:]
    count = own.shape[0] - 2
    span = count * rows * cols
    rank = lax.axis_index("dp")
    first = rank % CORES == 0
    for i, (here, there) in enumerate(((own, mate_own), (other, mate_other))):
        at = slice(i * cols, (i + 1) * cols)
        for out, window, near, far, swapped in (
            (mine, here, there, outer, 0),
            (mate, there, here, mate_outer, 1),
        ):
            low, high = live_bounds(offsets, span, rank ^ swapped, i)
            left_far = first if swapped == 0 else jnp.logical_not(first)
            before = place_of(rows, cols, 0) < low
            after = place_of(rows, cols, span - rows * cols) >= high
            far_end = far[i].astype(f32)
            left = jnp.where(left_far, far_end, near[count + 1].astype(f32))
            right = jnp.where(left_far, near[0].astype(f32), far_end)
            out[0, :, at] = jnp.where(before, left, window[1].astype(f32)).astype(bf16)
            out[1 : count - 1, :, at] = window[2:count]
            out[count - 1, :, at] = jnp.where(after, right, window[count].astype(f32)).astype(bf16)


def patch_states_kernel(offsets, leaving, staying, inner, outer, out_leaving, out_staying):
    _, half, rows, cols = leaving.shape
    span = 2 * half * rows * cols
    low, high = live_bounds(offsets, span, lax.axis_index("dp"), 0)
    first = lax.axis_index("dp") % CORES == 0
    group = lax.axis_index("group")
    for tile, states, out in ((1 - group, leaving, out_leaving), (group, staying, out_staying)):
        before = place_of(rows, cols, tile * (span // 2)) < low
        after = place_of(rows, cols, tile * (span // 2) + (half - 1) * rows * cols) >= high
        for i in range(3):
            near, far = inner[i].astype(f32), outer[i].astype(f32)
            left, right = jnp.where(first, far, near), jnp.where(first, near, far)
            out[i, 0] = jnp.where(before, left, states[i, 0]).astype(out.dtype)
            out[i, 1 : half - 1] = states[i, 1 : half - 1].astype(out.dtype)
            out[i, half - 1] = jnp.where(after, right, states[i, half - 1]).astype(out.dtype)


def part_kernel(pieces, *refs):
    mine, mate, out = refs[pieces:]
    rows = jnp.concatenate([r[...] for r in refs[:pieces]], axis=0)
    depth = mine.shape[0]
    value = jnp.dot(rows[:, :depth], mine[...], preferred_element_type=f32)
    value = value + jnp.dot(rows[:, depth:], mate[...], preferred_element_type=f32)
    out[...] = value.astype(out.dtype)


def part(pieces, weights, dtype, flops=0, after=()):
    rows = sum(p.shape[0] for p in pieces)
    cols = weights[0].shape[1]
    return call(
        functools.partial(part_kernel, len(pieces)),
        shape((rows, cols), dtype),
        *pieces,
        *weights,
        flops=flops or 2 * rows * pieces[0].shape[1] * cols,
        after=after,
    )


def own_order(rows, cols):
    tensors, groups = lax.axis_size("tensor"), lax.axis_size("group")
    share, wide = rows // tensors, cols // groups
    for j in range(tensors):
        row = pl.multiple_of((lax.axis_index("tensor") ^ j) * share, share)
        for i in range(groups):
            col = pl.multiple_of((lax.axis_index("group") ^ i) * wide, wide)
            here = (slice(j * share, (j + 1) * share), slice(i * wide, (i + 1) * wide))
            yield here, (pl.ds(row, share), pl.ds(col, wide)), row


def live_kernel(counts, cotangent, out):
    live = counts[lax.axis_index("dp") * lax.axis_size("group") + lax.axis_index("group")]
    for here, there, first_row in own_order(*cotangent.shape):
        value = cotangent[there].astype(f32)
        row = first_row + lax.broadcasted_iota(jnp.int32, value.shape, 0)
        out[here] = jnp.where(row < live, value, 0.0).astype(bf16)


def delta_kernel(*refs):
    own, (cotangent, activated, delta) = refs[0], refs[-3:]
    preact = own[...]
    for r in refs[1:-3]:
        preact = preact + r[...].astype(f32)
    sigmoid = 1.0 / (1.0 + jnp.exp(-preact))
    activated[...] = (preact * sigmoid).astype(bf16)
    derivative = sigmoid * (1.0 + preact * (1.0 - sigmoid))
    delta[...] = (cotangent[...].astype(f32) * derivative).astype(bf16)


def natural_kernel(value, out):
    for here, there, _ in own_order(*value.shape):
        out[there] = value[here]


def place_kernel(value, out):
    out[...] = value[...]


def zero_kernel(out):
    out[...] = jnp.zeros(out.shape, out.dtype)


def gather_kernel(*refs):
    start = 0
    for r in refs[:-1]:
        refs[-1][start : start + r.shape[0]] = r[...]
        start += r.shape[0]


def gradient_kernel(second, tokens, *refs):
    deltas, out = refs[:-1], refs[-1]
    depth = tokens.shape[1] // CORES
    value = lax.dot_general(
        tokens[:, depth * second : depth * (second + 1)],
        jnp.concatenate([r[...] for r in deltas], axis=0),
        (((0,), (0,)), ((), ())),
        preferred_element_type=f32,
    ).astype(out.dtype)
    tile = out.shape[1]
    for i in range(out.shape[0]):
        out[i] = value[i * tile : (i + 1) * tile]


def core_sum_kernel(mine, received, keep, send):
    group = lax.axis_index("group")
    cols = keep.shape[1] // 2
    keep[...] = mine[group] + received[group].astype(f32)
    value = (mine[1 - group] + received[1 - group].astype(f32)).astype(bf16)
    send[:, :cols] = value[:, cols:]
    send[:, cols:] = value[:, :cols]


def second_adam_kernel(staying, incoming, keep, back, master, moment, variance):
    _, half, rows, cols = staying.shape
    group = lax.axis_index("group")
    for k in range(half):
        for i, states in enumerate((staying, incoming)):
            here = (slice(k * rows, (k + 1) * rows), slice(i * cols, (i + 1) * cols))
            there = pl.ds(pl.multiple_of((group ^ i) * cols, cols), cols)
            gradient = keep[here] + back[here].astype(f32)
            values = [states[j, k].astype(f32) for j in range(3)]
            result = adam_update(*values, gradient, second_step)
            for ref, value in zip((master, moment, variance), result, strict=True):
                ref[k * rows : (k + 1) * rows, there] = value


def local(tokens, cotangent, counts, old_offsets, old_master, old_moment, old_variance, old_grad):
    ranks = lax.axis_size("dp")
    chips = ranks // CORES
    groups = lax.axis_size("group")
    tensors = lax.axis_size("tensor")
    rank = lax.axis_index("dp")
    chip, core = rank // CORES, rank % CORES
    tensor = lax.axis_index("tensor")
    slots, width = tokens.shape
    cols = cotangent.shape[1]
    old_cols = cols // groups
    depth = width // chips
    half = depth // CORES
    share = slots // tensors

    length = old_master.shape[2]
    margin = length // 10
    windows = [
        w.reshape(10, margin // LANES, LANES)
        for w in (old_master, old_moment, old_variance, old_grad)
    ]
    ahead = call(zero_kernel, shape((8, LANES), f32), flops=LONG)
    count, rows = windows[0].shape[0] - 2, windows[0].shape[1] * LANES // old_cols
    window = call(
        first_weights_kernel, shape((count + 2, rows, old_cols), bf16), *windows, after=[ahead]
    )

    def token_block(of_chip, of_tensor):
        return jnp.concatenate(
            [
                lax.dynamic_slice(
                    tokens, (of_tensor * share, of_chip * depth + (core ^ i) * half), (share, half)
                )
                for i in range(CORES)
            ],
            axis=1,
        )

    def blocks_of(steps, after):
        if half % LANES == 0 and share % 16 == 0:
            return token_blocks(tokens, steps, share, depth, after)
        return [
            jnp.concatenate(
                [
                    token_block(chip ^ step, tensor ^ j)
                    for j in range(tensors if step < DIRECT else 1)
                ]
            )
            for step in steps
        ]

    leaving_blocks = blocks_of(range(1, chips), [])

    cleared = call(place_kernel, shape(window.shape[1:], bf16), window[0], flops=LONG)
    other = swap(window, "group", 1)
    arrived = [swap(b, "dp", step * CORES) for step, b in enumerate(leaving_blocks, 1)]
    arrived = [lax.optimization_barrier((a, cleared))[0] for a in arrived]

    mate_window = swap(window, "dp", 1)
    tile = shape((3, count // 2, rows, old_cols), f32)
    leaving, staying, ends = call(
        first_states_kernel,
        [tile, tile, shape((2, 3, 1, rows, old_cols), bf16)],
        *windows,
        after=[mate_window],
    )

    ends = jnp.concatenate([ends[:, :, 0], jnp.stack([other[0], other[-1]])[:, None]], axis=1)
    inner = swap(jnp.where(core == 0, ends[1], ends[0]), "dp", 1)
    outer = swap_border(jnp.where(core == 0, ends[0], ends[1]))

    turned = call(
        live_kernel, shape((slots, cols), bf16), counts, cotangent, scalars=1, after=[other]
    )
    blocks = [[b] for b in [*blocks_of(range(1), [other]), *arrived]]
    for block in blocks[DIRECT:]:
        block += [swap(block[0], "tensor", j) for j in range(1, tensors)]

    far, _ = lax.optimization_barrier((jnp.stack([outer[0], outer[3]]), blocks[DIRECT]))

    mates = [mate_window] + [swap(w, "dp", 1) for w in (other, far)]
    weights = call(
        patch_weights_kernel,
        [shape((count, rows, cols), bf16)] * 2,
        old_offsets,
        window,
        other,
        *mates[:2],
        far,
        mates[2],
        scalars=1,
    )
    weights = [w.reshape(half, cols) for w in weights]

    steps = range(chips - 1, 0, -1)
    parts = []
    for step in steps:
        parts.append(part(blocks[step], weights, bf16, after=parts[-1:]))
    back = [swap(p, "dp", step * CORES) for step, p in zip(steps, parts, strict=True)]

    leaving, staying = call(
        patch_states_kernel,
        [shape(leaving.shape, bf16), shape(leaving.shape, f32)],
        old_offsets,
        leaving,
        staying,
        inner,
        outer,
        scalars=1,
        after=parts[-1:],
    )
    incoming = swap(leaving, "group", 1)
    own_block = blocks[0][0]
    total = part([own_block], weights, f32, LONG)
    activated, delta = call(
        delta_kernel, [shape((slots, cols), bf16)] * 2, total, *back, turned
    )

    deltas = [delta] + [swap(delta, "dp", step * CORES) for step in steps]

    flat = [p for step in (0, *steps) for p in blocks[step]]
    gathered = call(
        gather_kernel,
        shape((chips * slots, depth), bf16),
        *flat,
        flops=LONG,
        after=[incoming, delta],
    )
    flops = 2 * half * cols * chips * slots
    tile = half // groups
    to_mate, mine = (
        call(
            functools.partial(gradient_kernel, second),
            shape((groups, tile, cols), dtype),
            gathered,
            *deltas,
            flops=flops,
        )
        for second, dtype in ((1, bf16), (0, f32))
    )
    keep, send = call(
        core_sum_kernel,
        [shape((tile, cols), f32), shape((tile, cols), bf16)],
        mine,
        swap(to_mate, "dp", 1),
    )
    new = call(
        second_adam_kernel,
        [shape((tile, cols), f32)] * 3,
        staying,
        incoming,
        keep,
        swap(send, "group", 1),
    )
    activated = call(natural_kernel, shape((slots, cols), bf16), activated)
    return (activated, *new)


def solution(mesh):
    rows = P(("dp", "group"), "tensor")
    window = P(("tensor", "group"), "dp", None)
    return jax.shard_map(
        local,
        mesh=mesh,
        in_specs=(P(("dp", "group"), None), rows, P(), P(), window, window, window, window),
        out_specs=(rows, rows, rows, rows),
        check_vma=False,
    )
```

```python
import functools

import jax
import jax.numpy as jnp
from jax import lax
from jax.experimental import pallas as pl
from jax.experimental.pallas import tpu as pltpu
from jax.sharding import PartitionSpec as P

beta_one = 0.9
beta_two = 0.95
epsilon = 1e-08
learn_rate = 0.001
weight_decay = 0.1
first_step = 3.0
second_step = 4.0

LANES = 128
CORES = 2
f32, bf16 = jnp.float32, jnp.bfloat16
VMEM = 16 * 2**20
CUTS = 2
LAST = 1
DIRECT = 2
LONG = 10**11


def swap(value, axis, bits):
    pairs = [(source, source ^ bits) for source in range(lax.axis_size(axis))]
    return lax.ppermute(value, axis, pairs)


def swap_border(value):
    pairs = []
    for right in range(CORES, lax.axis_size("dp"), CORES):
        pairs += [(right - 1, right), (right, right - 1)]
    return lax.ppermute(value, "dp", pairs)


def adam_update(master, moment, variance, gradient, step_count):
    moment = beta_one * moment + (1.0 - beta_one) * gradient
    variance = beta_two * variance + (1.0 - beta_two) * gradient * gradient
    fix_one = 1.0 / (1.0 - beta_one**step_count)
    fix_two = 1.0 / (1.0 - beta_two**step_count)
    update = moment * fix_one / (jnp.sqrt(variance * fix_two) + epsilon) + weight_decay * master
    return (master - learn_rate * update, moment, variance)


def call(kernel, shapes, *args, scalars=0, flops=0, after=()):
    whole = pl.BlockSpec(memory_space=pltpu.VMEM)
    small = pl.BlockSpec(memory_space=pltpu.SMEM)
    touched = sum(a.size * a.dtype.itemsize for a in args)
    end = len(args)

    def body(*refs):
        kernel(*refs[:end], *refs[end + len(after) :])

    return pl.pallas_call(
        body,
        out_shape=shapes,
        in_specs=[small] * scalars
        + [whole] * (end - scalars)
        + [pl.BlockSpec(memory_space=pl.ANY)] * len(after),
        out_specs=jax.tree.map(lambda _: whole, shapes),
        compiler_params=pltpu.CompilerParams(vmem_limit_bytes=VMEM),
        cost_estimate=pl.CostEstimate(flops=flops, bytes_accessed=touched, transcendentals=0),
    )(*args, *after)


def shape(dims, dtype):
    return jax.ShapeDtypeStruct(dims, dtype)


def blocks_kernel(plan, skip, tokens, *refs):
    outs, sems = refs[skip:-1], refs[-1]
    rank, tensor = lax.axis_index("dp"), lax.axis_index("tensor")
    chip, core = rank // CORES, rank % CORES
    share = tokens.shape[0] // lax.axis_size("tensor")
    copies = []
    for (step, start), out in zip(plan, outs, strict=True):
        depth = out.shape[1] // CORES
        size = min(out.shape[0], share)
        for j in range(out.shape[0] // size):
            row = pl.multiple_of((tensor ^ j) * share + start, size)
            for i in range(CORES):
                col = pl.multiple_of(((chip ^ step) * CORES + (core ^ i)) * depth, depth)
                copies.append(
                    pltpu.make_async_copy(
                        tokens.at[pl.ds(row, size), pl.ds(col, depth)],
                        out.at[pl.ds(j * size, size), pl.ds(i * depth, depth)],
                        sems.at[len(copies)],
                    )
                )
    for copy in copies:
        copy.start()
    for copy in copies:
        copy.wait()


def token_blocks(tokens, plan, sizes, depth, after):
    outs = [shape((size, depth), bf16) for size in sizes]
    share = tokens.shape[0] // lax.axis_size("tensor")
    copies = sum(CORES * max(1, size // share) for size in sizes)
    return pl.pallas_call(
        functools.partial(blocks_kernel, plan, len(after)),
        out_shape=outs,
        in_specs=[pl.BlockSpec(memory_space=pl.ANY)] * (1 + len(after)),
        out_specs=[pl.BlockSpec(memory_space=pltpu.VMEM)] * len(outs),
        scratch_shapes=[pltpu.SemaphoreType.DMA((copies,))],
        compiler_params=pltpu.CompilerParams(vmem_limit_bytes=VMEM),
        cost_estimate=pl.CostEstimate(flops=0, bytes_accessed=10**6, transcendentals=0),
    )(tokens, *after)


def updated(windows, block, h, rows, per):
    picks = pl.ds(h, rows, stride=per) if per > 1 else pl.ds(0, rows)
    return adam_update(*[w[block, picks, :] for w in windows], first_step)


def first_weights_kernel(*refs):
    windows, out = refs[:4], refs[4]
    blocks, rows, cols = out.shape
    per = cols // LANES
    for k in range(blocks):
        for h in range(per):
            value = updated(windows, k, h, rows, per)[0]
            out[k, :, h * LANES : (h + 1) * LANES] = value.astype(bf16)


def first_states_kernel(*refs):
    windows, (leaving, staying, ends) = refs[:4], refs[4:]
    group = lax.axis_index("group")
    _, half, rows, cols = staying.shape
    per = cols // LANES
    runs = [(ends.at[0], 0, 1), (ends.at[1], 2 * half + 1, 1)]
    runs += [(leaving, (1 - group) * half + 1, half), (staying, group * half + 1, half)]
    for out, start, size in runs:
        for k in range(size):
            for h in range(per):
                values = updated(windows, start + k, h, rows, per)
                for i in range(3):
                    out[i, k, :, h * LANES : (h + 1) * LANES] = values[i].astype(out.dtype)


def live_bounds(offsets, span, rank, other):
    slab = lax.axis_index("tensor") * lax.axis_size("group") + (lax.axis_index("group") ^ other)
    start = rank * span
    return offsets[slab, rank] - start, offsets[slab, rank + 1] - start


def place_of(rows, cols, first):
    place = lax.broadcasted_iota(jnp.int32, (rows, cols), 0) * cols
    return first + place + lax.broadcasted_iota(jnp.int32, (rows, cols), 1)


def patch_weights_kernel(offsets, own, other, mate_own, mate_other, outer, mate_outer, mine, mate):
    rows, cols = own.shape[1:]
    count = own.shape[0] - 2
    span = count * rows * cols
    rank = lax.axis_index("dp")
    first = rank % CORES == 0
    for i, (here, there) in enumerate(((own, mate_own), (other, mate_other))):
        at = slice(i * cols, (i + 1) * cols)
        for out, window, near, far, swapped in (
            (mine, here, there, outer, 0),
            (mate, there, here, mate_outer, 1),
        ):
            low, high = live_bounds(offsets, span, rank ^ swapped, i)
            left_far = first if swapped == 0 else jnp.logical_not(first)
            before = place_of(rows, cols, 0) < low
            after = place_of(rows, cols, span - rows * cols) >= high
            far_end = far[i].astype(f32)
            left = jnp.where(left_far, far_end, near[count + 1].astype(f32))
            right = jnp.where(left_far, near[0].astype(f32), far_end)
            out[0, :, at] = jnp.where(before, left, window[1].astype(f32)).astype(bf16)
            out[1 : count - 1, :, at] = window[2:count]
            out[count - 1, :, at] = jnp.where(after, right, window[count].astype(f32)).astype(bf16)


def patch_states_kernel(offsets, leaving, staying, inner, outer, out_leaving, out_staying):
    _, half, rows, cols = leaving.shape
    span = 2 * half * rows * cols
    low, high = live_bounds(offsets, span, lax.axis_index("dp"), 0)
    first = lax.axis_index("dp") % CORES == 0
    group = lax.axis_index("group")
    for tile, states, out in ((1 - group, leaving, out_leaving), (group, staying, out_staying)):
        before = place_of(rows, cols, tile * (span // 2)) < low
        after = place_of(rows, cols, tile * (span // 2) + (half - 1) * rows * cols) >= high
        for i in range(3):
            near, far = inner[i].astype(f32), outer[i].astype(f32)
            left, right = jnp.where(first, far, near), jnp.where(first, near, far)
            out[i, 0] = jnp.where(before, left, states[i, 0]).astype(out.dtype)
            out[i, 1 : half - 1] = states[i, 1 : half - 1].astype(out.dtype)
            out[i, half - 1] = jnp.where(after, right, states[i, half - 1]).astype(out.dtype)


def part_kernel(pieces, *refs):
    mine, mate, out = refs[pieces:]
    rows = jnp.concatenate([r[...] for r in refs[:pieces]], axis=0)
    depth = mine.shape[0]
    value = jnp.dot(rows[:, :depth], mine[...], preferred_element_type=f32)
    value = value + jnp.dot(rows[:, depth:], mate[...], preferred_element_type=f32)
    out[...] = value.astype(out.dtype)


def part(pieces, weights, dtype, flops=0, after=()):
    rows = sum(p.shape[0] for p in pieces)
    cols = weights[0].shape[1]
    return call(
        functools.partial(part_kernel, len(pieces)),
        shape((rows, cols), dtype),
        *pieces,
        *weights,
        flops=flops or 2 * rows * pieces[0].shape[1] * cols,
        after=after,
    )


def own_order(rows, cols):
    tensors, groups = lax.axis_size("tensor"), lax.axis_size("group")
    share, wide = rows // tensors, cols // groups
    for j in range(tensors):
        row = pl.multiple_of((lax.axis_index("tensor") ^ j) * share, share)
        for i in range(groups):
            col = pl.multiple_of((lax.axis_index("group") ^ i) * wide, wide)
            here = (slice(j * share, (j + 1) * share), slice(i * wide, (i + 1) * wide))
            yield here, (pl.ds(row, share), pl.ds(col, wide)), row


def live_kernel(counts, cotangent, out):
    live = counts[lax.axis_index("dp") * lax.axis_size("group") + lax.axis_index("group")]
    for here, there, first_row in own_order(*cotangent.shape):
        value = cotangent[there].astype(f32)
        row = first_row + lax.broadcasted_iota(jnp.int32, value.shape, 0)
        out[here] = jnp.where(row < live, value, 0.0).astype(bf16)


def delta_kernel(*refs):
    own, (cotangent, activated, delta) = refs[0], refs[-3:]
    preact = own[...]
    for r in refs[1:-3]:
        preact = preact + r[...].astype(f32)
    sigmoid = 1.0 / (1.0 + jnp.exp(-preact))
    activated[...] = (preact * sigmoid).astype(bf16)
    derivative = sigmoid * (1.0 + preact * (1.0 - sigmoid))
    delta[...] = (cotangent[...].astype(f32) * derivative).astype(bf16)


def natural_kernel(value, out):
    for here, there, _ in own_order(*value.shape):
        out[there] = value[here]


def place_kernel(value, out):
    out[...] = value[...]


def zero_kernel(out):
    out[...] = jnp.zeros(out.shape, out.dtype)


def gather_kernel(*refs):
    start = 0
    for r in refs[:-1]:
        refs[-1][start : start + r.shape[0]] = r[...]
        start += r.shape[0]


def mate_gradient_kernel(tokens, *refs):
    deltas, (first, second) = refs[:-2], refs[-2:]
    depth = tokens.shape[1] // CORES
    value = lax.dot_general(
        tokens[:, depth:],
        jnp.concatenate([r[...] for r in deltas], axis=0),
        (((0,), (0,)), ((), ())),
        preferred_element_type=f32,
    )
    tile = first.shape[0]
    low = lax.axis_index("group") == 0
    first[...] = jnp.where(low, value[tile:], value[:tile]).astype(bf16)
    second[...] = jnp.where(low, value[:tile], value[tile:]).astype(bf16)


def own_gradient_kernel(tokens, *refs):
    deltas, out = refs[:-1], refs[-1]
    depth = tokens.shape[1] // CORES
    value = lax.dot_general(
        tokens[:, :depth],
        jnp.concatenate([r[...] for r in deltas], axis=0),
        (((0,), (0,)), ((), ())),
        preferred_element_type=f32,
    )
    tile = out.shape[1]
    for i in range(out.shape[0]):
        out[i] = value[i * tile : (i + 1) * tile]


def send_kernel(mine, received, *outs):
    other = 1 - lax.axis_index("group")
    cols = received.shape[1] // 2
    rows = outs[0].shape[0]
    for i, out in enumerate(outs):
        at = slice(i * rows, (i + 1) * rows)
        value = (mine[other, at] + received[at].astype(f32)).astype(bf16)
        out[:, :cols] = value[:, cols:]
        out[:, cols:] = value[:, :cols]


def second_adam_kernel(cut, staying, incoming, mine, received, back, *refs):
    outs, results, sems = refs[-7:-4], refs[-4:-1], refs[-1]
    _, half, rows, cols = staying.shape
    group = lax.axis_index("group")
    size = back.shape[0] // rows
    for k in range(size):
        block = cut * size + k
        for i, states in enumerate((staying, incoming)):
            at = slice(i * cols, (i + 1) * cols)
            there = pl.ds(pl.multiple_of((group ^ i) * cols, cols), cols)
            tile_rows = slice(block * rows, (block + 1) * rows)
            here = slice(k * rows, (k + 1) * rows)
            gradient = mine[group, tile_rows, at] + received[tile_rows, at].astype(f32)
            gradient = gradient + back[here, at].astype(f32)
            values = [states[j, block].astype(f32) for j in range(3)]
            result = adam_update(*values, gradient, second_step)
            for ref, value in zip(results, result, strict=True):
                ref[here, there] = value
    total = back.shape[0]
    copies = [
        pltpu.make_async_copy(ref, out.at[pl.ds(cut * total, total)], sems.at[i])
        for i, (ref, out) in enumerate(zip(results, outs, strict=True))
    ]
    for copy in copies:
        copy.start()
    for copy in copies:
        copy.wait()


def second_adam(cut, staying, incoming, mine, received, back, done):
    rows, cols = received.shape
    whole = pl.BlockSpec(memory_space=pltpu.VMEM)
    anywhere = pl.BlockSpec(memory_space=pl.ANY)
    return pl.pallas_call(
        functools.partial(second_adam_kernel, cut),
        out_shape=[shape((rows, cols), f32)] * 3,
        in_specs=[whole] * 5 + [anywhere] * len(done),
        out_specs=[anywhere] * 3,
        scratch_shapes=[pltpu.VMEM(back.shape, f32)] * 3 + [pltpu.SemaphoreType.DMA((3,))],
        input_output_aliases={5 + i: i for i in range(len(done))},
        compiler_params=pltpu.CompilerParams(vmem_limit_bytes=VMEM),
        cost_estimate=pl.CostEstimate(flops=0, bytes_accessed=10**6, transcendentals=0),
    )(staying, incoming, mine, received, back, *done)


def local(tokens, cotangent, counts, old_offsets, old_master, old_moment, old_variance, old_grad):
    ranks = lax.axis_size("dp")
    chips = ranks // CORES
    groups = lax.axis_size("group")
    tensors = lax.axis_size("tensor")
    rank = lax.axis_index("dp")
    chip, core = rank // CORES, rank % CORES
    tensor = lax.axis_index("tensor")
    slots, width = tokens.shape
    cols = cotangent.shape[1]
    old_cols = cols // groups
    depth = width // chips
    half = depth // CORES
    share = slots // tensors

    length = old_master.shape[2]
    margin = length // 10
    windows = [
        w.reshape(10, margin // LANES, LANES)
        for w in (old_master, old_moment, old_variance, old_grad)
    ]
    ahead = call(zero_kernel, shape((8, LANES), f32), flops=LONG)
    count, rows = windows[0].shape[0] - 2, windows[0].shape[1] * LANES // old_cols
    window = call(
        first_weights_kernel, shape((count + 2, rows, old_cols), bf16), *windows, after=[ahead]
    )

    aligned = half % LANES == 0 and share % 16 == 0
    last = share // LAST if aligned and share % (16 * LAST) == 0 else share
    plan = [(step, 0) for step in range(1, chips - 1)]
    plan += [(chips - 1, start) for start in range(0, share, last)]
    sizes = [slots if step < DIRECT else share for step in range(1, chips - 1)]
    sizes += [last] * (share // last)

    def blocks_of(plan, sizes, after):
        if aligned:
            return token_blocks(tokens, plan, sizes, depth, after)
        return [
            jnp.concatenate(
                [
                    jnp.concatenate(
                        [
                            lax.dynamic_slice(
                                tokens,
                                (
                                    (tensor ^ j) * share + start,
                                    (chip ^ step) * depth + (core ^ i) * half,
                                ),
                                (min(size, share), half),
                            )
                            for i in range(CORES)
                        ],
                        axis=1,
                    )
                    for j in range(max(1, size // share))
                ]
            )
            for (step, start), size in zip(plan, sizes, strict=True)
        ]

    other = swap(window, "group", 1)
    leaving_blocks = blocks_of(plan, sizes, [])
    arrived = [
        (step, swap(b, "dp", step * CORES))
        for (step, _), b in zip(plan, leaving_blocks, strict=True)
    ]

    mate_window = swap(window, "dp", 1)
    tile = shape((3, count // 2, rows, old_cols), f32)
    leaving, staying, ends = call(
        first_states_kernel,
        [tile, tile, shape((2, 3, 1, rows, old_cols), bf16)],
        *windows,
        after=leaving_blocks[:1],
    )

    ends = jnp.concatenate([ends[:, :, 0], jnp.stack([other[0], other[-1]])[:, None]], axis=1)
    inner = swap(jnp.where(core == 0, ends[1], ends[0]), "dp", 1)
    outer = swap_border(jnp.where(core == 0, ends[0], ends[1]))

    turned = call(
        live_kernel, shape((slots, cols), bf16), counts, cotangent, scalars=1, after=[other]
    )
    blocks = [blocks_of([(0, 0)], [slots], [other])]
    for step in range(1, chips):
        block = [b for at, b in arrived if at == step]
        if step >= DIRECT:
            block += [swap(b, "tensor", j) for j in range(1, tensors) for b in list(block)]
        blocks.append(block)

    far, _ = lax.optimization_barrier((jnp.stack([outer[0], outer[3]]), blocks[DIRECT]))

    mates = [mate_window] + [swap(w, "dp", 1) for w in (other, far)]
    weights = call(
        patch_weights_kernel,
        [shape((count, rows, cols), bf16)] * 2,
        old_offsets,
        window,
        other,
        *mates[:2],
        far,
        mates[2],
        scalars=1,
    )
    weights = [w.reshape(half, cols) for w in weights]

    steps = range(chips - 1, 0, -1)
    parts = []
    for step in steps:
        parts.append(part(blocks[step], weights, bf16, after=parts[-1:]))
    back = [swap(p, "dp", step * CORES) for step, p in zip(steps, parts, strict=True)]

    leaving, staying = call(
        patch_states_kernel,
        [shape(leaving.shape, bf16), shape(leaving.shape, f32)],
        old_offsets,
        leaving,
        staying,
        inner,
        outer,
        scalars=1,
        after=parts[-1:],
    )
    incoming = swap(leaving, "group", 1)
    own_block = blocks[0][0]
    total = part([own_block], weights, f32, LONG)
    activated, delta = call(
        delta_kernel, [shape((slots, cols), bf16)] * 2, total, *back, turned
    )

    deltas = [delta] + [swap(delta, "dp", step * CORES) for step in range(1, chips)]

    flat = [p for step in range(chips) for p in blocks[step]]
    gathered = call(
        gather_kernel,
        shape((chips * slots, depth), bf16),
        *flat,
        flops=LONG,
        after=[incoming, delta],
    )
    flops = 2 * half * cols * chips * slots
    tile = half // groups
    cuts = CUTS if tile % (CUTS * 16) == 0 and leaving.shape[1] % CUTS == 0 else 1
    first, second = call(
        mate_gradient_kernel, [shape((tile, cols), bf16)] * 2, gathered, *deltas, flops=flops
    )
    first = swap(first, "dp", 1)
    mine = call(own_gradient_kernel, shape((groups, tile, cols), f32), gathered, *deltas, flops=flops)
    second = swap(second, "dp", 1)
    sends = call(send_kernel, [shape((tile // cuts, cols), bf16)] * cuts, mine, first)
    new = []
    for cut, send in enumerate(sends):
        new = second_adam(cut, staying, incoming, mine, second, swap(send, "group", 1), new)
    activated = call(natural_kernel, shape((slots, cols), bf16), activated)
    return (activated, *new)


def solution(mesh):
    rows = P(("dp", "group"), "tensor")
    window = P(("tensor", "group"), "dp", None)
    return jax.shard_map(
        local,
        mesh=mesh,
        in_specs=(P(("dp", "group"), None), rows, P(), P(), window, window, window, window),
        out_specs=(rows, rows, rows, rows),
        check_vma=False,
    )
```

```python
import functools

import jax
import jax.numpy as jnp
from jax import lax
from jax.experimental import pallas as pl
from jax.experimental.pallas import tpu as pltpu
from jax.sharding import PartitionSpec as P

beta_one = 0.9
beta_two = 0.95
epsilon = 1e-08
learn_rate = 0.001
weight_decay = 0.1
first_step = 3.0
second_step = 4.0

LANES = 128
CORES = 2
f32, bf16 = jnp.float32, jnp.bfloat16
VMEM = 16 * 2**20
CUTS = 2
LAST = 1
DIRECT = 1
LONG = 10**11


def swap(value, axis, bits):
    pairs = [(source, source ^ bits) for source in range(lax.axis_size(axis))]
    return lax.ppermute(value, axis, pairs)


def swap_border(value):
    pairs = []
    for right in range(CORES, lax.axis_size("dp"), CORES):
        pairs += [(right - 1, right), (right, right - 1)]
    return lax.ppermute(value, "dp", pairs)


def adam_update(master, moment, variance, gradient, step_count):
    moment = beta_one * moment + (1.0 - beta_one) * gradient
    variance = beta_two * variance + (1.0 - beta_two) * gradient * gradient
    fix_one = 1.0 / (1.0 - beta_one**step_count)
    fix_two = 1.0 / (1.0 - beta_two**step_count)
    update = moment * fix_one / (jnp.sqrt(variance * fix_two) + epsilon) + weight_decay * master
    return (master - learn_rate * update, moment, variance)


def call(kernel, shapes, *args, scalars=0, flops=0, after=()):
    whole = pl.BlockSpec(memory_space=pltpu.VMEM)
    small = pl.BlockSpec(memory_space=pltpu.SMEM)
    touched = sum(a.size * a.dtype.itemsize for a in args)
    end = len(args)

    def body(*refs):
        kernel(*refs[:end], *refs[end + len(after) :])

    return pl.pallas_call(
        body,
        out_shape=shapes,
        in_specs=[small] * scalars
        + [whole] * (end - scalars)
        + [pl.BlockSpec(memory_space=pl.ANY)] * len(after),
        out_specs=jax.tree.map(lambda _: whole, shapes),
        compiler_params=pltpu.CompilerParams(vmem_limit_bytes=VMEM),
        cost_estimate=pl.CostEstimate(flops=flops, bytes_accessed=touched, transcendentals=0),
    )(*args, *after)


def shape(dims, dtype):
    return jax.ShapeDtypeStruct(dims, dtype)


def blocks_kernel(plan, skip, tokens, *refs):
    outs, sems = refs[skip:-1], refs[-1]
    rank, tensor = lax.axis_index("dp"), lax.axis_index("tensor")
    chip, core = rank // CORES, rank % CORES
    share = tokens.shape[0] // lax.axis_size("tensor")
    copies = []
    for (step, start), out in zip(plan, outs, strict=True):
        depth = out.shape[1] // CORES
        size = min(out.shape[0], share)
        for j in range(out.shape[0] // size):
            row = pl.multiple_of((tensor ^ j) * share + start, size)
            for i in range(CORES):
                col = pl.multiple_of(((chip ^ step) * CORES + (core ^ i)) * depth, depth)
                copies.append(
                    pltpu.make_async_copy(
                        tokens.at[pl.ds(row, size), pl.ds(col, depth)],
                        out.at[pl.ds(j * size, size), pl.ds(i * depth, depth)],
                        sems.at[len(copies)],
                    )
                )
    for copy in copies:
        copy.start()
    for copy in copies:
        copy.wait()


def token_blocks(tokens, plan, sizes, depth, after):
    outs = [shape((size, depth), bf16) for size in sizes]
    share = tokens.shape[0] // lax.axis_size("tensor")
    copies = sum(CORES * max(1, size // share) for size in sizes)
    return pl.pallas_call(
        functools.partial(blocks_kernel, plan, len(after)),
        out_shape=outs,
        in_specs=[pl.BlockSpec(memory_space=pl.ANY)] * (1 + len(after)),
        out_specs=[pl.BlockSpec(memory_space=pltpu.VMEM)] * len(outs),
        scratch_shapes=[pltpu.SemaphoreType.DMA((copies,))],
        compiler_params=pltpu.CompilerParams(vmem_limit_bytes=VMEM),
        cost_estimate=pl.CostEstimate(flops=0, bytes_accessed=10**6, transcendentals=0),
    )(tokens, *after)


def updated(windows, block, h, rows, per):
    picks = pl.ds(h, rows, stride=per) if per > 1 else pl.ds(0, rows)
    return adam_update(*[w[block, picks, :] for w in windows], first_step)


def first_weights_kernel(*refs):
    windows, out, ends = refs[:4], refs[4], refs[5]
    blocks, rows, cols = out.shape
    per = cols // LANES
    for k in range(blocks):
        for h in range(per):
            at = slice(h * LANES, (h + 1) * LANES)
            values = updated(windows, k, h, rows, per)
            out[k, :, at] = values[0].astype(bf16)
            if k in (0, blocks - 1):
                for i in range(2):
                    ends[min(k, 1), i, :, at] = values[i + 1].astype(bf16)


def border_kernel(window, other, ends, to_mate, to_next):
    first = lax.axis_index("dp") % CORES == 0
    last = window.shape[0] - 1
    pairs = [(window[0], window[last]), (other[0], other[last])]
    pairs += [(ends[0, i], ends[1, i]) for i in range(2)]
    for i, (head, tail) in enumerate(pairs):
        head, tail = head.astype(f32), tail.astype(f32)
        to_mate[i] = jnp.where(first, tail, head).astype(bf16)
        to_next[i] = jnp.where(first, head, tail).astype(bf16)


def live_bounds(offsets, span, rank, other):
    slab = lax.axis_index("tensor") * lax.axis_size("group") + (lax.axis_index("group") ^ other)
    start = rank * span
    return offsets[slab, rank] - start, offsets[slab, rank + 1] - start


def place_of(rows, cols, first):
    place = lax.broadcasted_iota(jnp.int32, (rows, cols), 0) * cols
    return first + place + lax.broadcasted_iota(jnp.int32, (rows, cols), 1)


def patch_weights_kernel(offsets, own, other, mate_own, mate_other, outer, mate_outer, mine, mate):
    rows, cols = own.shape[1:]
    count = own.shape[0] - 2
    span = count * rows * cols
    rank = lax.axis_index("dp")
    first = rank % CORES == 0
    for i, (here, there) in enumerate(((own, mate_own), (other, mate_other))):
        at = slice(i * cols, (i + 1) * cols)
        for out, window, near, far, swapped in (
            (mine, here, there, outer, 0),
            (mate, there, here, mate_outer, 1),
        ):
            low, high = live_bounds(offsets, span, rank ^ swapped, i)
            left_far = first if swapped == 0 else jnp.logical_not(first)
            before = place_of(rows, cols, 0) < low
            after = place_of(rows, cols, span - rows * cols) >= high
            far_end = far[i].astype(f32)
            left = jnp.where(left_far, far_end, near[count + 1].astype(f32))
            right = jnp.where(left_far, near[0].astype(f32), far_end)
            out[0, :, at] = jnp.where(before, left, window[1].astype(f32)).astype(bf16)
            out[1 : count - 1, :, at] = window[2:count]
            out[count - 1, :, at] = jnp.where(after, right, window[count].astype(f32)).astype(bf16)


def states_kernel(offsets, *refs):
    windows, (inner, outer), outs = refs[:4], refs[4:6], refs[6:]
    _, half, rows, cols = outs[0].shape
    per = cols // LANES
    span = 2 * half * rows * cols
    low, high = live_bounds(offsets, span, lax.axis_index("dp"), 0)
    first = lax.axis_index("dp") % CORES == 0
    group = lax.axis_index("group")
    for tile, out in zip((1 - group, group), outs, strict=True):
        for k in range(half):
            block = tile * half + k
            for h in range(per):
                at = slice(h * LANES, (h + 1) * LANES)
                values = updated(windows, block + 1, h, rows, per)
                place = lax.broadcasted_iota(jnp.int32, (rows, LANES), 0) * cols
                place = place + lax.broadcasted_iota(jnp.int32, (rows, LANES), 1)
                place = place + (block * rows * cols + h * LANES)
                for i in range(3):
                    value = values[i]
                    at_end = (0, 2, 3)[i]
                    near = inner[at_end, :, at].astype(f32)
                    far = outer[at_end, :, at].astype(f32)
                    if k == 0:
                        value = jnp.where(place < low, jnp.where(first, far, near), value)
                    if k == half - 1:
                        value = jnp.where(place >= high, jnp.where(first, near, far), value)
                    out[i, k, :, at] = value.astype(out.dtype)


def part_kernel(pieces, *refs):
    mine, mate, out = refs[pieces:]
    rows = jnp.concatenate([r[...] for r in refs[:pieces]], axis=0)
    depth = mine.shape[0]
    value = jnp.dot(rows[:, :depth], mine[...], preferred_element_type=f32)
    value = value + jnp.dot(rows[:, depth:], mate[...], preferred_element_type=f32)
    out[...] = value.astype(out.dtype)


def part(pieces, weights, dtype, flops=0, after=()):
    rows = sum(p.shape[0] for p in pieces)
    cols = weights[0].shape[1]
    return call(
        functools.partial(part_kernel, len(pieces)),
        shape((rows, cols), dtype),
        *pieces,
        *weights,
        flops=flops or 2 * rows * pieces[0].shape[1] * cols,
        after=after,
    )


def own_order(rows, cols):
    tensors, groups = lax.axis_size("tensor"), lax.axis_size("group")
    share, wide = rows // tensors, cols // groups
    for j in range(tensors):
        row = pl.multiple_of((lax.axis_index("tensor") ^ j) * share, share)
        for i in range(groups):
            col = pl.multiple_of((lax.axis_index("group") ^ i) * wide, wide)
            here = (slice(j * share, (j + 1) * share), slice(i * wide, (i + 1) * wide))
            yield here, (pl.ds(row, share), pl.ds(col, wide)), row


def live_kernel(counts, cotangent, out):
    live = counts[lax.axis_index("dp") * lax.axis_size("group") + lax.axis_index("group")]
    for here, there, first_row in own_order(*cotangent.shape):
        value = cotangent[there].astype(f32)
        row = first_row + lax.broadcasted_iota(jnp.int32, value.shape, 0)
        out[here] = jnp.where(row < live, value, 0.0).astype(bf16)


def delta_kernel(*refs):
    own, (cotangent, activated, delta) = refs[0], refs[-3:]
    preact = own[...]
    for r in refs[1:-3]:
        preact = preact + r[...].astype(f32)
    sigmoid = 1.0 / (1.0 + jnp.exp(-preact))
    activated[...] = (preact * sigmoid).astype(bf16)
    derivative = sigmoid * (1.0 + preact * (1.0 - sigmoid))
    delta[...] = (cotangent[...].astype(f32) * derivative).astype(bf16)


def natural_kernel(value, out):
    for here, there, _ in own_order(*value.shape):
        out[there] = value[here]


def place_kernel(value, out):
    out[...] = value[...]


def zero_kernel(out):
    out[...] = jnp.zeros(out.shape, out.dtype)


def gather_kernel(*refs):
    start = 0
    for r in refs[:-1]:
        refs[-1][start : start + r.shape[0]] = r[...]
        start += r.shape[0]


def mate_gradient_kernel(tokens, *refs):
    deltas, (first, second) = refs[:-2], refs[-2:]
    depth = tokens.shape[1] // CORES
    value = lax.dot_general(
        tokens[:, depth:],
        jnp.concatenate([r[...] for r in deltas], axis=0),
        (((0,), (0,)), ((), ())),
        preferred_element_type=f32,
    )
    tile = first.shape[0]
    low = lax.axis_index("group") == 0
    first[...] = jnp.where(low, value[tile:], value[:tile]).astype(bf16)
    second[...] = jnp.where(low, value[:tile], value[tile:]).astype(bf16)


def own_gradient_kernel(tokens, *refs):
    deltas, out = refs[:-1], refs[-1]
    depth = tokens.shape[1] // CORES
    value = lax.dot_general(
        tokens[:, :depth],
        jnp.concatenate([r[...] for r in deltas], axis=0),
        (((0,), (0,)), ((), ())),
        preferred_element_type=f32,
    )
    tile = out.shape[1]
    for i in range(out.shape[0]):
        out[i] = value[i * tile : (i + 1) * tile]


def send_kernel(mine, received, *outs):
    other = 1 - lax.axis_index("group")
    cols = received.shape[1] // 2
    rows = outs[0].shape[0]
    for i, out in enumerate(outs):
        at = slice(i * rows, (i + 1) * rows)
        value = (mine[other, at] + received[at].astype(f32)).astype(bf16)
        out[:, :cols] = value[:, cols:]
        out[:, cols:] = value[:, :cols]


def second_adam_kernel(cut, staying, incoming, mine, received, back, *refs):
    outs, results, sems = refs[-7:-4], refs[-4:-1], refs[-1]
    _, half, rows, cols = staying.shape
    group = lax.axis_index("group")
    size = back.shape[0] // rows
    for k in range(size):
        block = cut * size + k
        for i, states in enumerate((staying, incoming)):
            at = slice(i * cols, (i + 1) * cols)
            there = pl.ds(pl.multiple_of((group ^ i) * cols, cols), cols)
            tile_rows = slice(block * rows, (block + 1) * rows)
            here = slice(k * rows, (k + 1) * rows)
            gradient = mine[group, tile_rows, at] + received[tile_rows, at].astype(f32)
            gradient = gradient + back[here, at].astype(f32)
            values = [states[j, block].astype(f32) for j in range(3)]
            result = adam_update(*values, gradient, second_step)
            for ref, value in zip(results, result, strict=True):
                ref[here, there] = value
    total = back.shape[0]
    copies = [
        pltpu.make_async_copy(ref, out.at[pl.ds(cut * total, total)], sems.at[i])
        for i, (ref, out) in enumerate(zip(results, outs, strict=True))
    ]
    for copy in copies:
        copy.start()
    for copy in copies:
        copy.wait()


def second_adam(cut, staying, incoming, mine, received, back, done):
    rows, cols = received.shape
    whole = pl.BlockSpec(memory_space=pltpu.VMEM)
    anywhere = pl.BlockSpec(memory_space=pl.ANY)
    return pl.pallas_call(
        functools.partial(second_adam_kernel, cut),
        out_shape=[shape((rows, cols), f32)] * 3,
        in_specs=[whole] * 5 + [anywhere] * len(done),
        out_specs=[anywhere] * 3,
        scratch_shapes=[pltpu.VMEM(back.shape, f32)] * 3 + [pltpu.SemaphoreType.DMA((3,))],
        input_output_aliases={5 + i: i for i in range(len(done))},
        compiler_params=pltpu.CompilerParams(vmem_limit_bytes=VMEM),
        cost_estimate=pl.CostEstimate(flops=0, bytes_accessed=10**6, transcendentals=0),
    )(staying, incoming, mine, received, back, *done)


def local(tokens, cotangent, counts, old_offsets, old_master, old_moment, old_variance, old_grad):
    ranks = lax.axis_size("dp")
    chips = ranks // CORES
    groups = lax.axis_size("group")
    tensors = lax.axis_size("tensor")
    rank = lax.axis_index("dp")
    chip, core = rank // CORES, rank % CORES
    tensor = lax.axis_index("tensor")
    slots, width = tokens.shape
    cols = cotangent.shape[1]
    old_cols = cols // groups
    depth = width // chips
    half = depth // CORES
    share = slots // tensors

    length = old_master.shape[2]
    margin = length // 10
    windows = [
        w.reshape(10, margin // LANES, LANES)
        for w in (old_master, old_moment, old_variance, old_grad)
    ]
    aligned = half % LANES == 0 and share % 16 == 0
    last = share // LAST if aligned and share % (16 * LAST) == 0 else share
    plan = [(step, 0) for step in range(1, chips - 1)]
    plan += [(chips - 1, start) for start in range(0, share, last)]
    sizes = [slots if step < DIRECT else share for step in range(1, chips - 1)]
    sizes += [last] * (share // last)

    def blocks_of(plan, sizes, after):
        if aligned:
            return token_blocks(tokens, plan, sizes, depth, after)
        return [
            jnp.concatenate(
                [
                    jnp.concatenate(
                        [
                            lax.dynamic_slice(
                                tokens,
                                (
                                    (tensor ^ j) * share + start,
                                    (chip ^ step) * depth + (core ^ i) * half,
                                ),
                                (min(size, share), half),
                            )
                            for i in range(CORES)
                        ],
                        axis=1,
                    )
                    for j in range(max(1, size // share))
                ]
            )
            for (step, start), size in zip(plan, sizes, strict=True)
        ]

    ahead = call(zero_kernel, shape((8, LANES), f32), flops=LONG)
    leaving_blocks = blocks_of(plan, sizes, [ahead])
    count, rows = windows[0].shape[0] - 2, windows[0].shape[1] * LANES // old_cols
    window, ends = call(
        first_weights_kernel,
        [shape((count + 2, rows, old_cols), bf16), shape((2, 2, rows, old_cols), bf16)],
        *windows,
        after=leaving_blocks[:1],
    )

    other = swap(window, "group", 1)
    arrived = [
        (step, swap(b, "dp", step * CORES))
        for (step, _), b in zip(plan, leaving_blocks, strict=True)
    ]

    mate_window = swap(window, "dp", 1)
    to_mate, to_next = call(
        border_kernel,
        [shape((4, rows, old_cols), bf16)] * 2,
        window,
        other,
        ends,
        after=[mate_window],
        flops=3 * 10**9,
    )
    inner, outer = swap(to_mate, "dp", 1), swap_border(to_next)

    turned = call(
        live_kernel, shape((slots, cols), bf16), counts, cotangent, scalars=1, after=[other]
    )
    blocks = [blocks_of([(0, 0)], [slots], [other])]
    for step in range(1, chips):
        block = [b for at, b in arrived if at == step]
        if step >= DIRECT:
            block += [swap(b, "tensor", j) for j in range(1, tensors) for b in list(block)]
        blocks.append(block)

    far, _ = lax.optimization_barrier((outer[:2], blocks[DIRECT]))

    mates = [mate_window] + [swap(w, "dp", 1) for w in (other, far)]
    weights = call(
        patch_weights_kernel,
        [shape((count, rows, cols), bf16)] * 2,
        old_offsets,
        window,
        other,
        *mates[:2],
        far,
        mates[2],
        scalars=1,
    )
    weights = [w.reshape(half, cols) for w in weights]

    steps = [chips - 1, *range(1, chips - 1)]
    parts = []
    for step in steps:
        parts.append(part(blocks[step], weights, bf16, after=parts[-1:]))
    back = [swap(p, "dp", step * CORES) for step, p in zip(steps, parts, strict=True)]

    leaving, staying = call(
        states_kernel,
        [shape((3, count // groups, rows, old_cols), dtype) for dtype in (bf16, f32)],
        old_offsets,
        *windows,
        inner,
        outer,
        scalars=1,
        after=parts[-1:],
    )
    incoming = swap(leaving, "group", 1)
    own_block = blocks[0][0]
    total = part([own_block], weights, f32, LONG)
    activated, delta = call(
        delta_kernel, [shape((slots, cols), bf16)] * 2, total, *back, turned
    )

    deltas = [delta] + [swap(delta, "dp", step * CORES) for step in range(1, chips)]

    flat = [p for step in range(chips) for p in blocks[step]]
    gathered = call(
        gather_kernel,
        shape((chips * slots, depth), bf16),
        *flat,
        flops=LONG,
        after=[incoming, delta],
    )
    flops = 2 * half * cols * chips * slots
    tile = half // groups
    cuts = CUTS if tile % (CUTS * 16) == 0 and leaving.shape[1] % CUTS == 0 else 1
    first, second = call(
        mate_gradient_kernel, [shape((tile, cols), bf16)] * 2, gathered, *deltas, flops=flops
    )
    first = swap(first, "dp", 1)
    mine = call(own_gradient_kernel, shape((groups, tile, cols), f32), gathered, *deltas, flops=flops)
    second = swap(second, "dp", 1)
    sends = call(send_kernel, [shape((tile // cuts, cols), bf16)] * cuts, mine, first)
    new = []
    for cut, send in enumerate(sends):
        new = second_adam(cut, staying, incoming, mine, second, swap(send, "group", 1), new)
    activated = call(natural_kernel, shape((slots, cols), bf16), activated)
    return (activated, *new)


def solution(mesh):
    rows = P(("dp", "group"), "tensor")
    window = P(("tensor", "group"), "dp", None)
    return jax.shard_map(
        local,
        mesh=mesh,
        in_specs=(P(("dp", "group"), None), rows, P(), P(), window, window, window, window),
        out_specs=(rows, rows, rows, rows),
        check_vma=False,
    )
```

```python
import functools

import jax
import jax.numpy as jnp
from jax import lax
from jax.experimental import pallas as pl
from jax.experimental.pallas import tpu as pltpu
from jax.sharding import PartitionSpec as P

beta_one = 0.9
beta_two = 0.95
epsilon = 1e-08
learn_rate = 0.001
weight_decay = 0.1
first_step = 3.0
second_step = 4.0

LANES = 128
CORES = 2
f32, bf16 = jnp.float32, jnp.bfloat16
VMEM = 16 * 2**20
CUTS = 4
LAST = 1
DIRECT = 1
LONG = 10**11


def swap(value, axis, bits):
    pairs = [(source, source ^ bits) for source in range(lax.axis_size(axis))]
    return lax.ppermute(value, axis, pairs)


def swap_border(value):
    pairs = []
    for right in range(CORES, lax.axis_size("dp"), CORES):
        pairs += [(right - 1, right), (right, right - 1)]
    return lax.ppermute(value, "dp", pairs)


def adam_update(master, moment, variance, gradient, step_count):
    moment = beta_one * moment + (1.0 - beta_one) * gradient
    variance = beta_two * variance + (1.0 - beta_two) * gradient * gradient
    fix_one = 1.0 / (1.0 - beta_one**step_count)
    fix_two = 1.0 / (1.0 - beta_two**step_count)
    update = moment * fix_one / (jnp.sqrt(variance * fix_two) + epsilon) + weight_decay * master
    return (master - learn_rate * update, moment, variance)


def call(kernel, shapes, *args, scalars=0, flops=0, after=()):
    whole = pl.BlockSpec(memory_space=pltpu.VMEM)
    small = pl.BlockSpec(memory_space=pltpu.SMEM)
    touched = sum(a.size * a.dtype.itemsize for a in args)
    end = len(args)

    def body(*refs):
        kernel(*refs[:end], *refs[end + len(after) :])

    return pl.pallas_call(
        body,
        out_shape=shapes,
        in_specs=[small] * scalars
        + [whole] * (end - scalars)
        + [pl.BlockSpec(memory_space=pl.ANY)] * len(after),
        out_specs=jax.tree.map(lambda _: whole, shapes),
        compiler_params=pltpu.CompilerParams(vmem_limit_bytes=VMEM),
        cost_estimate=pl.CostEstimate(flops=flops, bytes_accessed=touched, transcendentals=0),
    )(*args, *after)


def shape(dims, dtype):
    return jax.ShapeDtypeStruct(dims, dtype)


def blocks_kernel(plan, skip, tokens, *refs):
    outs, sems = refs[skip:-1], refs[-1]
    rank, tensor = lax.axis_index("dp"), lax.axis_index("tensor")
    chip, core = rank // CORES, rank % CORES
    share = tokens.shape[0] // lax.axis_size("tensor")
    copies = []
    for (step, start), out in zip(plan, outs, strict=True):
        depth = out.shape[1] // CORES
        size = min(out.shape[0], share)
        for j in range(out.shape[0] // size):
            row = pl.multiple_of((tensor ^ j) * share + start, size)
            for i in range(CORES):
                col = pl.multiple_of(((chip ^ step) * CORES + (core ^ i)) * depth, depth)
                copies.append(
                    pltpu.make_async_copy(
                        tokens.at[pl.ds(row, size), pl.ds(col, depth)],
                        out.at[pl.ds(j * size, size), pl.ds(i * depth, depth)],
                        sems.at[len(copies)],
                    )
                )
    for copy in copies:
        copy.start()
    for copy in copies:
        copy.wait()


def token_blocks(tokens, plan, sizes, depth, after):
    outs = [shape((size, depth), bf16) for size in sizes]
    share = tokens.shape[0] // lax.axis_size("tensor")
    copies = sum(CORES * max(1, size // share) for size in sizes)
    return pl.pallas_call(
        functools.partial(blocks_kernel, plan, len(after)),
        out_shape=outs,
        in_specs=[pl.BlockSpec(memory_space=pl.ANY)] * (1 + len(after)),
        out_specs=[pl.BlockSpec(memory_space=pltpu.VMEM)] * len(outs),
        scratch_shapes=[pltpu.SemaphoreType.DMA((copies,))],
        compiler_params=pltpu.CompilerParams(vmem_limit_bytes=VMEM),
        cost_estimate=pl.CostEstimate(flops=0, bytes_accessed=10**6, transcendentals=0),
    )(tokens, *after)


def updated(windows, block, h, rows, per):
    picks = pl.ds(h, rows, stride=per) if per > 1 else pl.ds(0, rows)
    return adam_update(*[w[block, picks, :] for w in windows], first_step)


def first_weights_kernel(*refs):
    windows, out, ends = refs[:4], refs[4], refs[5]
    blocks, rows, cols = out.shape
    per = cols // LANES
    for k in range(blocks):
        for h in range(per):
            at = slice(h * LANES, (h + 1) * LANES)
            values = updated(windows, k, h, rows, per)
            out[k, :, at] = values[0].astype(bf16)
            if k in (0, blocks - 1):
                for i in range(2):
                    ends[min(k, 1), i, :, at] = values[i + 1].astype(bf16)


def border_kernel(window, other, ends, to_mate, to_next):
    first = lax.axis_index("dp") % CORES == 0
    last = window.shape[0] - 1
    pairs = [(window[0], window[last]), (other[0], other[last])]
    pairs += [(ends[0, i], ends[1, i]) for i in range(2)]
    for i, (head, tail) in enumerate(pairs):
        head, tail = head.astype(f32), tail.astype(f32)
        to_mate[i] = jnp.where(first, tail, head).astype(bf16)
        to_next[i] = jnp.where(first, head, tail).astype(bf16)


def live_bounds(offsets, span, rank, other):
    slab = lax.axis_index("tensor") * lax.axis_size("group") + (lax.axis_index("group") ^ other)
    start = rank * span
    return offsets[slab, rank] - start, offsets[slab, rank + 1] - start


def place_of(rows, cols, first):
    place = lax.broadcasted_iota(jnp.int32, (rows, cols), 0) * cols
    return first + place + lax.broadcasted_iota(jnp.int32, (rows, cols), 1)


def patch_weights_kernel(offsets, own, other, mate_own, mate_other, outer, mate_outer, mine, mate):
    rows, cols = own.shape[1:]
    count = own.shape[0] - 2
    span = count * rows * cols
    rank = lax.axis_index("dp")
    first = rank % CORES == 0
    for i, (here, there) in enumerate(((own, mate_own), (other, mate_other))):
        at = slice(i * cols, (i + 1) * cols)
        for out, window, near, far, swapped in (
            (mine, here, there, outer, 0),
            (mate, there, here, mate_outer, 1),
        ):
            low, high = live_bounds(offsets, span, rank ^ swapped, i)
            left_far = first if swapped == 0 else jnp.logical_not(first)
            before = place_of(rows, cols, 0) < low
            after = place_of(rows, cols, span - rows * cols) >= high
            far_end = far[i].astype(f32)
            left = jnp.where(left_far, far_end, near[count + 1].astype(f32))
            right = jnp.where(left_far, near[0].astype(f32), far_end)
            out[0, :, at] = jnp.where(before, left, window[1].astype(f32)).astype(bf16)
            out[1 : count - 1, :, at] = window[2:count]
            out[count - 1, :, at] = jnp.where(after, right, window[count].astype(f32)).astype(bf16)


def states_kernel(offsets, *refs):
    windows, (inner, outer), outs = refs[:4], refs[4:6], refs[6:]
    _, half, rows, cols = outs[0].shape
    per = cols // LANES
    span = 2 * half * rows * cols
    low, high = live_bounds(offsets, span, lax.axis_index("dp"), 0)
    first = lax.axis_index("dp") % CORES == 0
    group = lax.axis_index("group")
    for tile, out in zip((1 - group, group), outs, strict=True):
        for k in range(half):
            block = tile * half + k
            for h in range(per):
                at = slice(h * LANES, (h + 1) * LANES)
                values = updated(windows, block + 1, h, rows, per)
                place = lax.broadcasted_iota(jnp.int32, (rows, LANES), 0) * cols
                place = place + lax.broadcasted_iota(jnp.int32, (rows, LANES), 1)
                place = place + (block * rows * cols + h * LANES)
                for i in range(3):
                    value = values[i]
                    at_end = (0, 2, 3)[i]
                    near = inner[at_end, :, at].astype(f32)
                    far = outer[at_end, :, at].astype(f32)
                    if k == 0:
                        value = jnp.where(place < low, jnp.where(first, far, near), value)
                    if k == half - 1:
                        value = jnp.where(place >= high, jnp.where(first, near, far), value)
                    out[i, k, :, at] = value.astype(out.dtype)


def part_kernel(pieces, *refs):
    mine, mate, out = refs[pieces:]
    rows = jnp.concatenate([r[...] for r in refs[:pieces]], axis=0)
    depth = mine.shape[0]
    value = jnp.dot(rows[:, :depth], mine[...], preferred_element_type=f32)
    value = value + jnp.dot(rows[:, depth:], mate[...], preferred_element_type=f32)
    out[...] = value.astype(out.dtype)


def part(pieces, weights, dtype, flops=0, after=()):
    rows = sum(p.shape[0] for p in pieces)
    cols = weights[0].shape[1]
    return call(
        functools.partial(part_kernel, len(pieces)),
        shape((rows, cols), dtype),
        *pieces,
        *weights,
        flops=flops or 2 * rows * pieces[0].shape[1] * cols,
        after=after,
    )


def own_order(rows, cols):
    tensors, groups = lax.axis_size("tensor"), lax.axis_size("group")
    share, wide = rows // tensors, cols // groups
    for j in range(tensors):
        row = pl.multiple_of((lax.axis_index("tensor") ^ j) * share, share)
        for i in range(groups):
            col = pl.multiple_of((lax.axis_index("group") ^ i) * wide, wide)
            here = (slice(j * share, (j + 1) * share), slice(i * wide, (i + 1) * wide))
            yield here, (pl.ds(row, share), pl.ds(col, wide)), row


def live_kernel(counts, cotangent, out):
    live = counts[lax.axis_index("dp") * lax.axis_size("group") + lax.axis_index("group")]
    for here, there, first_row in own_order(*cotangent.shape):
        value = cotangent[there].astype(f32)
        row = first_row + lax.broadcasted_iota(jnp.int32, value.shape, 0)
        out[here] = jnp.where(row < live, value, 0.0).astype(bf16)


def delta_kernel(*refs):
    own, (cotangent, activated, delta) = refs[0], refs[-3:]
    preact = own[...]
    for r in refs[1:-3]:
        preact = preact + r[...].astype(f32)
    sigmoid = 1.0 / (1.0 + jnp.exp(-preact))
    activated[...] = (preact * sigmoid).astype(bf16)
    derivative = sigmoid * (1.0 + preact * (1.0 - sigmoid))
    delta[...] = (cotangent[...].astype(f32) * derivative).astype(bf16)


def natural_kernel(value, out):
    for here, there, _ in own_order(*value.shape):
        out[there] = value[here]


def zero_kernel(out):
    out[...] = jnp.zeros(out.shape, out.dtype)


def gather_kernel(*refs):
    start = 0
    for r in refs[:-1]:
        refs[-1][start : start + r.shape[0]] = r[...]
        start += r.shape[0]


def mate_gradient_kernel(tokens, *refs):
    deltas, (first, second) = refs[:-2], refs[-2:]
    depth = tokens.shape[1] // CORES
    value = lax.dot_general(
        tokens[:, depth:],
        jnp.concatenate([r[...] for r in deltas], axis=0),
        (((0,), (0,)), ((), ())),
        preferred_element_type=f32,
    )
    tile = first.shape[0]
    low = lax.axis_index("group") == 0
    first[...] = jnp.where(low, value[tile:], value[:tile]).astype(bf16)
    second[...] = jnp.where(low, value[:tile], value[tile:]).astype(bf16)


def own_gradient_kernel(tokens, *refs):
    deltas, out = refs[:-1], refs[-1]
    depth = tokens.shape[1] // CORES
    value = lax.dot_general(
        tokens[:, :depth],
        jnp.concatenate([r[...] for r in deltas], axis=0),
        (((0,), (0,)), ((), ())),
        preferred_element_type=f32,
    )
    tile = out.shape[1]
    for i in range(out.shape[0]):
        out[i] = value[i * tile : (i + 1) * tile]


def send_kernel(mine, received, *outs):
    other = 1 - lax.axis_index("group")
    cols = received.shape[1] // 2
    rows = outs[0].shape[0]
    for i, out in enumerate(outs):
        at = slice(i * rows, (i + 1) * rows)
        value = (mine[other, at] + received[at].astype(f32)).astype(bf16)
        out[:, :cols] = value[:, cols:]
        out[:, cols:] = value[:, :cols]


def second_adam_kernel(cut, staying, incoming, mine, received, back, *refs):
    outs, results, sems = refs[-7:-4], refs[-4:-1], refs[-1]
    _, half, rows, cols = staying.shape
    group = lax.axis_index("group")
    size = back.shape[0] // rows
    for k in range(size):
        block = cut * size + k
        for i, states in enumerate((staying, incoming)):
            at = slice(i * cols, (i + 1) * cols)
            there = pl.ds(pl.multiple_of((group ^ i) * cols, cols), cols)
            tile_rows = slice(block * rows, (block + 1) * rows)
            here = slice(k * rows, (k + 1) * rows)
            gradient = mine[group, tile_rows, at] + received[tile_rows, at].astype(f32)
            gradient = gradient + back[here, at].astype(f32)
            values = [states[j, block].astype(f32) for j in range(3)]
            result = adam_update(*values, gradient, second_step)
            for ref, value in zip(results, result, strict=True):
                ref[here, there] = value
    total = back.shape[0]
    copies = [
        pltpu.make_async_copy(ref, out.at[pl.ds(cut * total, total)], sems.at[i])
        for i, (ref, out) in enumerate(zip(results, outs, strict=True))
    ]
    for copy in copies:
        copy.start()
    for copy in copies:
        copy.wait()


def second_adam(cut, staying, incoming, mine, received, back, done):
    rows, cols = received.shape
    whole = pl.BlockSpec(memory_space=pltpu.VMEM)
    anywhere = pl.BlockSpec(memory_space=pl.ANY)
    return pl.pallas_call(
        functools.partial(second_adam_kernel, cut),
        out_shape=[shape((rows, cols), f32)] * 3,
        in_specs=[whole] * 5 + [anywhere] * len(done),
        out_specs=[anywhere] * 3,
        scratch_shapes=[pltpu.VMEM(back.shape, f32)] * 3 + [pltpu.SemaphoreType.DMA((3,))],
        input_output_aliases={5 + i: i for i in range(len(done))},
        compiler_params=pltpu.CompilerParams(vmem_limit_bytes=VMEM),
        cost_estimate=pl.CostEstimate(flops=0, bytes_accessed=10**6, transcendentals=0),
    )(staying, incoming, mine, received, back, *done)


def local(tokens, cotangent, counts, old_offsets, old_master, old_moment, old_variance, old_grad):
    ranks = lax.axis_size("dp")
    chips = ranks // CORES
    groups = lax.axis_size("group")
    tensors = lax.axis_size("tensor")
    rank = lax.axis_index("dp")
    chip, core = rank // CORES, rank % CORES
    tensor = lax.axis_index("tensor")
    slots, width = tokens.shape
    cols = cotangent.shape[1]
    old_cols = cols // groups
    depth = width // chips
    half = depth // CORES
    share = slots // tensors

    length = old_master.shape[2]
    margin = length // 10
    windows = [
        w.reshape(10, margin // LANES, LANES)
        for w in (old_master, old_moment, old_variance, old_grad)
    ]
    aligned = half % LANES == 0 and share % 16 == 0
    last = share // LAST if aligned and share % (16 * LAST) == 0 else share
    plan = [(step, 0) for step in range(1, chips - 1)]
    plan += [(chips - 1, start) for start in range(0, share, last)]
    sizes = [slots if step < DIRECT else share for step in range(1, chips - 1)]
    sizes += [last] * (share // last)

    def blocks_of(plan, sizes, after):
        if aligned:
            return token_blocks(tokens, plan, sizes, depth, after)
        return [
            jnp.concatenate(
                [
                    jnp.concatenate(
                        [
                            lax.dynamic_slice(
                                tokens,
                                (
                                    (tensor ^ j) * share + start,
                                    (chip ^ step) * depth + (core ^ i) * half,
                                ),
                                (min(size, share), half),
                            )
                            for i in range(CORES)
                        ],
                        axis=1,
                    )
                    for j in range(max(1, size // share))
                ]
            )
            for (step, start), size in zip(plan, sizes, strict=True)
        ]

    ahead = call(zero_kernel, shape((8, LANES), f32), flops=LONG)
    leaving_blocks = blocks_of(plan, sizes, [ahead])
    count, rows = windows[0].shape[0] - 2, windows[0].shape[1] * LANES // old_cols
    window, ends = call(
        first_weights_kernel,
        [shape((count + 2, rows, old_cols), bf16), shape((2, 2, rows, old_cols), bf16)],
        *windows,
        after=leaving_blocks[:1],
    )

    other = swap(window, "group", 1)
    arrived = [
        (step, swap(b, "dp", step * CORES))
        for (step, _), b in zip(plan, leaving_blocks, strict=True)
    ]

    mate_window = swap(window, "dp", 1)

    to_mate, to_next = call(
        border_kernel,
        [shape((4, rows, old_cols), bf16)] * 2,
        window,
        other,
        ends,
        after=[mate_window],
        flops=3 * 10**9,
    )
    inner, outer = swap(to_mate, "dp", 1), swap_border(to_next)

    turned = call(
        live_kernel, shape((slots, cols), bf16), counts, cotangent, scalars=1, after=[other]
    )
    blocks = [blocks_of([(0, 0)], [slots], [other])]
    for step in range(1, chips):
        block = [b for at, b in arrived if at == step]
        if step >= DIRECT:
            block += [swap(b, "tensor", j) for j in range(1, tensors) for b in list(block)]
        blocks.append(block)

    far, _ = lax.optimization_barrier((outer[:2], blocks[DIRECT]))

    mates = [mate_window] + [swap(w, "dp", 1) for w in (other, far)]
    weights = call(
        patch_weights_kernel,
        [shape((count, rows, cols), bf16)] * 2,
        old_offsets,
        window,
        other,
        *mates[:2],
        far,
        mates[2],
        scalars=1,
    )
    weights = [w.reshape(half, cols) for w in weights]

    steps = [chips - 1, *range(1, chips - 1)]
    parts = []
    for step in steps:
        parts.append(part(blocks[step], weights, bf16, after=parts[-1:]))
    back = [swap(p, "dp", step * CORES) for step, p in zip(steps, parts, strict=True)]

    leaving, staying = call(
        states_kernel,
        [shape((3, count // groups, rows, old_cols), dtype) for dtype in (bf16, f32)],
        old_offsets,
        *windows,
        inner,
        outer,
        scalars=1,
        after=parts[-1:],
    )
    incoming = swap(leaving, "group", 1)

    total = part(blocks[0], weights, f32, LONG)
    activated, delta = call(
        delta_kernel, [shape((slots, cols), bf16)] * 2, total, *back, turned
    )

    deltas = [delta] + [swap(delta, "dp", step * CORES) for step in steps]

    flat = [p for step in (0, *steps) for p in blocks[step]]
    gathered = call(
        gather_kernel,
        shape((chips * slots, depth), bf16),
        *flat,
        flops=LONG,
        after=[incoming, delta],
    )
    flops = 2 * half * cols * chips * slots
    tile = half // groups
    cuts = CUTS if tile % (CUTS * 16) == 0 and leaving.shape[1] % CUTS == 0 else 1
    first, second = call(
        mate_gradient_kernel, [shape((tile, cols), bf16)] * 2, gathered, *deltas, flops=flops
    )
    first = swap(first, "dp", 1)
    mine = call(own_gradient_kernel, shape((groups, tile, cols), f32), gathered, *deltas, flops=flops)
    second = swap(second, "dp", 1)
    sends = call(send_kernel, [shape((tile // cuts, cols), bf16)] * cuts, mine, first)
    new = []
    for cut, send in enumerate(sends):
        new = second_adam(cut, staying, incoming, mine, second, swap(send, "group", 1), new)
    activated = call(natural_kernel, shape((slots, cols), bf16), activated)
    return (activated, *new)


def solution(mesh):
    rows = P(("dp", "group"), "tensor")
    window = P(("tensor", "group"), "dp", None)
    return jax.shard_map(
        local,
        mesh=mesh,
        in_specs=(P(("dp", "group"), None), rows, P(), P(), window, window, window, window),
        out_specs=(rows, rows, rows, rows),
        check_vma=False,
    )
```

```python
import functools

import jax
import jax.numpy as jnp
from jax import lax
from jax.experimental import pallas as pl
from jax.experimental.pallas import tpu as pltpu
from jax.sharding import PartitionSpec as P

beta_one = 0.9
beta_two = 0.95
epsilon = 1e-08
learn_rate = 0.001
weight_decay = 0.1
first_step = 3.0
second_step = 4.0

LANES = 128
CORES = 2
f32, bf16 = jnp.float32, jnp.bfloat16
VMEM = 16 * 2**20
CUTS = 4
LAST = 1
DIRECT = 1
LONG = 10**11


def swap(value, axis, bits):
    pairs = [(source, source ^ bits) for source in range(lax.axis_size(axis))]
    return lax.ppermute(value, axis, pairs)


def swap_border(value):
    pairs = []
    for right in range(CORES, lax.axis_size("dp"), CORES):
        pairs += [(right - 1, right), (right, right - 1)]
    return lax.ppermute(value, "dp", pairs)


def adam_update(master, moment, variance, gradient, step_count):
    moment = beta_one * moment + (1.0 - beta_one) * gradient
    variance = beta_two * variance + (1.0 - beta_two) * gradient * gradient
    fix_one = 1.0 / (1.0 - beta_one**step_count)
    fix_two = 1.0 / (1.0 - beta_two**step_count)
    update = moment * fix_one / (jnp.sqrt(variance * fix_two) + epsilon) + weight_decay * master
    return (master - learn_rate * update, moment, variance)


def call(kernel, shapes, *args, scalars=0, flops=0, after=()):
    whole = pl.BlockSpec(memory_space=pltpu.VMEM)
    small = pl.BlockSpec(memory_space=pltpu.SMEM)
    touched = sum(a.size * a.dtype.itemsize for a in args)
    end = len(args)

    def body(*refs):
        kernel(*refs[:end], *refs[end + len(after) :])

    return pl.pallas_call(
        body,
        out_shape=shapes,
        in_specs=[small] * scalars
        + [whole] * (end - scalars)
        + [pl.BlockSpec(memory_space=pl.ANY)] * len(after),
        out_specs=jax.tree.map(lambda _: whole, shapes),
        compiler_params=pltpu.CompilerParams(vmem_limit_bytes=VMEM),
        cost_estimate=pl.CostEstimate(flops=flops, bytes_accessed=touched, transcendentals=0),
    )(*args, *after)


def shape(dims, dtype):
    return jax.ShapeDtypeStruct(dims, dtype)


def blocks_kernel(plan, skip, tokens, *refs):
    outs, sems = refs[skip:-1], refs[-1]
    rank, tensor = lax.axis_index("dp"), lax.axis_index("tensor")
    chip, core = rank // CORES, rank % CORES
    share = tokens.shape[0] // lax.axis_size("tensor")
    copies = []
    for (step, start), out in zip(plan, outs, strict=True):
        depth = out.shape[1] // CORES
        size = min(out.shape[0], share)
        for j in range(out.shape[0] // size):
            row = pl.multiple_of((tensor ^ j) * share + start, size)
            for i in range(CORES):
                col = pl.multiple_of(((chip ^ step) * CORES + (core ^ i)) * depth, depth)
                copies.append(
                    pltpu.make_async_copy(
                        tokens.at[pl.ds(row, size), pl.ds(col, depth)],
                        out.at[pl.ds(j * size, size), pl.ds(i * depth, depth)],
                        sems.at[len(copies)],
                    )
                )
    for copy in copies:
        copy.start()
    for copy in copies:
        copy.wait()


def token_blocks(tokens, plan, sizes, depth, after):
    outs = [shape((size, depth), bf16) for size in sizes]
    share = tokens.shape[0] // lax.axis_size("tensor")
    copies = sum(CORES * max(1, size // share) for size in sizes)
    return pl.pallas_call(
        functools.partial(blocks_kernel, plan, len(after)),
        out_shape=outs,
        in_specs=[pl.BlockSpec(memory_space=pl.ANY)] * (1 + len(after)),
        out_specs=[pl.BlockSpec(memory_space=pltpu.VMEM)] * len(outs),
        scratch_shapes=[pltpu.SemaphoreType.DMA((copies,))],
        compiler_params=pltpu.CompilerParams(vmem_limit_bytes=VMEM),
        cost_estimate=pl.CostEstimate(flops=0, bytes_accessed=10**6, transcendentals=0),
    )(tokens, *after)


def updated(windows, block, h, rows, per):
    picks = pl.ds(h, rows, stride=per) if per > 1 else pl.ds(0, rows)
    return adam_update(*[w[block, picks, :] for w in windows], first_step)


def first_weights_kernel(*refs):
    windows, out, ends = refs[:4], refs[4], refs[5]
    blocks, rows, cols = out.shape
    per = cols // LANES
    for k in range(blocks):
        for h in range(per):
            at = slice(h * LANES, (h + 1) * LANES)
            values = updated(windows, k, h, rows, per)
            out[k, :, at] = values[0].astype(bf16)
            if k in (0, blocks - 1):
                for i in range(2):
                    ends[min(k, 1), i, :, at] = values[i + 1].astype(bf16)


def border_kernel(window, other, ends, to_mate, to_next):
    first = lax.axis_index("dp") % CORES == 0
    last = window.shape[0] - 1
    pairs = [(window[0], window[last]), (other[0], other[last])]
    pairs += [(ends[0, i], ends[1, i]) for i in range(2)]
    for i, (head, tail) in enumerate(pairs):
        head, tail = head.astype(f32), tail.astype(f32)
        to_mate[i] = jnp.where(first, tail, head).astype(bf16)
        to_next[i] = jnp.where(first, head, tail).astype(bf16)


def live_bounds(offsets, span, rank, other):
    slab = lax.axis_index("tensor") * lax.axis_size("group") + (lax.axis_index("group") ^ other)
    start = rank * span
    return offsets[slab, rank] - start, offsets[slab, rank + 1] - start


def place_of(rows, cols, first):
    place = lax.broadcasted_iota(jnp.int32, (rows, cols), 0) * cols
    return first + place + lax.broadcasted_iota(jnp.int32, (rows, cols), 1)


def patch_weights_kernel(offsets, own, other, mate_own, mate_other, outer, mate_outer, mine, mate):
    rows, cols = own.shape[1:]
    count = own.shape[0] - 2
    span = count * rows * cols
    rank = lax.axis_index("dp")
    first = rank % CORES == 0
    for i, (here, there) in enumerate(((own, mate_own), (other, mate_other))):
        at = slice(i * cols, (i + 1) * cols)
        for out, window, near, far, swapped in (
            (mine, here, there, outer, 0),
            (mate, there, here, mate_outer, 1),
        ):
            low, high = live_bounds(offsets, span, rank ^ swapped, i)
            left_far = first if swapped == 0 else jnp.logical_not(first)
            before = place_of(rows, cols, 0) < low
            after = place_of(rows, cols, span - rows * cols) >= high
            far_end = far[i].astype(f32)
            left = jnp.where(left_far, far_end, near[count + 1].astype(f32))
            right = jnp.where(left_far, near[0].astype(f32), far_end)
            out[0, :, at] = jnp.where(before, left, window[1].astype(f32)).astype(bf16)
            out[1 : count - 1, :, at] = window[2:count]
            out[count - 1, :, at] = jnp.where(after, right, window[count].astype(f32)).astype(bf16)


def states_kernel(offsets, *refs):
    windows, (inner, outer), outs = refs[:4], refs[4:6], refs[6:]
    _, half, rows, cols = outs[0].shape
    per = cols // LANES
    span = 2 * half * rows * cols
    low, high = live_bounds(offsets, span, lax.axis_index("dp"), 0)
    first = lax.axis_index("dp") % CORES == 0
    group = lax.axis_index("group")
    for tile, out in zip((1 - group, group), outs, strict=True):
        for k in range(half):
            block = tile * half + k
            for h in range(per):
                at = slice(h * LANES, (h + 1) * LANES)
                values = updated(windows, block + 1, h, rows, per)
                place = lax.broadcasted_iota(jnp.int32, (rows, LANES), 0) * cols
                place = place + lax.broadcasted_iota(jnp.int32, (rows, LANES), 1)
                place = place + (block * rows * cols + h * LANES)
                for i in range(3):
                    value = values[i]
                    at_end = (0, 2, 3)[i]
                    near = inner[at_end, :, at].astype(f32)
                    far = outer[at_end, :, at].astype(f32)
                    if k == 0:
                        value = jnp.where(place < low, jnp.where(first, far, near), value)
                    if k == half - 1:
                        value = jnp.where(place >= high, jnp.where(first, near, far), value)
                    out[i, k, :, at] = value.astype(out.dtype)


def part_kernel(pieces, *refs):
    mine, mate, out = refs[pieces:]
    rows = jnp.concatenate([r[...] for r in refs[:pieces]], axis=0)
    depth = mine.shape[0]
    value = jnp.dot(rows[:, :depth], mine[...], preferred_element_type=f32)
    value = value + jnp.dot(rows[:, depth:], mate[...], preferred_element_type=f32)
    out[...] = value.astype(out.dtype)


def part(pieces, weights, dtype, flops=0, after=()):
    rows = sum(p.shape[0] for p in pieces)
    cols = weights[0].shape[1]
    return call(
        functools.partial(part_kernel, len(pieces)),
        shape((rows, cols), dtype),
        *pieces,
        *weights,
        flops=flops or 2 * rows * pieces[0].shape[1] * cols,
        after=after,
    )


def own_order(rows, cols):
    tensors, groups = lax.axis_size("tensor"), lax.axis_size("group")
    share, wide = rows // tensors, cols // groups
    for j in range(tensors):
        row = pl.multiple_of((lax.axis_index("tensor") ^ j) * share, share)
        for i in range(groups):
            col = pl.multiple_of((lax.axis_index("group") ^ i) * wide, wide)
            here = (slice(j * share, (j + 1) * share), slice(i * wide, (i + 1) * wide))
            yield here, (pl.ds(row, share), pl.ds(col, wide)), row


def live_kernel(counts, cotangent, out):
    live = counts[lax.axis_index("dp") * lax.axis_size("group") + lax.axis_index("group")]
    for here, there, first_row in own_order(*cotangent.shape):
        value = cotangent[there].astype(f32)
        row = first_row + lax.broadcasted_iota(jnp.int32, value.shape, 0)
        out[here] = jnp.where(row < live, value, 0.0).astype(bf16)


def delta_kernel(*refs):
    own, (cotangent, activated, delta) = refs[0], refs[-3:]
    preact = own[...]
    for r in refs[1:-3]:
        preact = preact + r[...].astype(f32)
    sigmoid = 1.0 / (1.0 + jnp.exp(-preact))
    activated[...] = (preact * sigmoid).astype(bf16)
    derivative = sigmoid * (1.0 + preact * (1.0 - sigmoid))
    delta[...] = (cotangent[...].astype(f32) * derivative).astype(bf16)


def natural_kernel(value, out):
    for here, there, _ in own_order(*value.shape):
        out[there] = value[here]


def zero_kernel(out):
    out[...] = jnp.zeros(out.shape, out.dtype)


def gather_kernel(*refs):
    start = 0
    for r in refs[:-1]:
        refs[-1][start : start + r.shape[0]] = r[...]
        start += r.shape[0]


def mate_gradient_kernel(tokens, *refs):
    deltas, (first, second) = refs[:-2], refs[-2:]
    depth = tokens.shape[1] // CORES
    value = lax.dot_general(
        tokens[:, depth:],
        jnp.concatenate([r[...] for r in deltas], axis=0),
        (((0,), (0,)), ((), ())),
        preferred_element_type=f32,
    )
    tile = first.shape[0]
    low = lax.axis_index("group") == 0
    first[...] = jnp.where(low, value[tile:], value[:tile]).astype(bf16)
    second[...] = jnp.where(low, value[:tile], value[tile:]).astype(bf16)


def own_gradient_kernel(tokens, *refs):
    deltas, out = refs[:-1], refs[-1]
    depth = tokens.shape[1] // CORES
    value = lax.dot_general(
        tokens[:, :depth],
        jnp.concatenate([r[...] for r in deltas], axis=0),
        (((0,), (0,)), ((), ())),
        preferred_element_type=f32,
    )
    tile = out.shape[1]
    for i in range(out.shape[0]):
        out[i] = value[i * tile : (i + 1) * tile]


def send_kernel(mine, received, *outs):
    other = 1 - lax.axis_index("group")
    cols = received.shape[1] // 2
    rows = outs[0].shape[0]
    for i, out in enumerate(outs):
        at = slice(i * rows, (i + 1) * rows)
        value = (mine[other, at] + received[at].astype(f32)).astype(bf16)
        out[:, :cols] = value[:, cols:]
        out[:, cols:] = value[:, :cols]


def second_adam_kernel(cut, staying, incoming, mine, received, back, *refs):
    outs, results, sems = refs[-7:-4], refs[-4:-1], refs[-1]
    _, half, rows, cols = staying.shape
    group = lax.axis_index("group")
    size = back.shape[0] // rows
    for k in range(size):
        block = cut * size + k
        for i, states in enumerate((staying, incoming)):
            at = slice(i * cols, (i + 1) * cols)
            there = pl.ds(pl.multiple_of((group ^ i) * cols, cols), cols)
            tile_rows = slice(block * rows, (block + 1) * rows)
            here = slice(k * rows, (k + 1) * rows)
            gradient = mine[group, tile_rows, at] + received[tile_rows, at].astype(f32)
            gradient = gradient + back[here, at].astype(f32)
            values = [states[j, block].astype(f32) for j in range(3)]
            result = adam_update(*values, gradient, second_step)
            for ref, value in zip(results, result, strict=True):
                ref[here, there] = value
    total = back.shape[0]
    copies = [
        pltpu.make_async_copy(ref, out.at[pl.ds(cut * total, total)], sems.at[i])
        for i, (ref, out) in enumerate(zip(results, outs, strict=True))
    ]
    for copy in copies:
        copy.start()
    for copy in copies:
        copy.wait()


def second_adam(cut, staying, incoming, mine, received, back, done):
    rows, cols = received.shape
    whole = pl.BlockSpec(memory_space=pltpu.VMEM)
    anywhere = pl.BlockSpec(memory_space=pl.ANY)
    return pl.pallas_call(
        functools.partial(second_adam_kernel, cut),
        out_shape=[shape((rows, cols), f32)] * 3,
        in_specs=[whole] * 5 + [anywhere] * len(done),
        out_specs=[anywhere] * 3,
        scratch_shapes=[pltpu.VMEM(back.shape, f32)] * 3 + [pltpu.SemaphoreType.DMA((3,))],
        input_output_aliases={5 + i: i for i in range(len(done))},
        compiler_params=pltpu.CompilerParams(vmem_limit_bytes=VMEM),
        cost_estimate=pl.CostEstimate(flops=0, bytes_accessed=10**6, transcendentals=0),
    )(staying, incoming, mine, received, back, *done)


def local(tokens, cotangent, counts, old_offsets, old_master, old_moment, old_variance, old_grad):
    ranks = lax.axis_size("dp")
    chips = ranks // CORES
    groups = lax.axis_size("group")
    tensors = lax.axis_size("tensor")
    rank = lax.axis_index("dp")
    chip, core = rank // CORES, rank % CORES
    tensor = lax.axis_index("tensor")
    slots, width = tokens.shape
    cols = cotangent.shape[1]
    old_cols = cols // groups
    depth = width // chips
    half = depth // CORES
    share = slots // tensors

    length = old_master.shape[2]
    margin = length // 10
    windows = [
        w.reshape(10, margin // LANES, LANES)
        for w in (old_master, old_moment, old_variance, old_grad)
    ]
    aligned = half % LANES == 0 and share % 16 == 0
    last = share // LAST if aligned and share % (16 * LAST) == 0 else share
    plan = [(step, 0) for step in range(1, chips - 1)]
    plan += [(chips - 1, start) for start in range(0, share, last)]
    sizes = [slots if step < DIRECT else share for step in range(1, chips - 1)]
    sizes += [last] * (share // last)

    def blocks_of(plan, sizes, after):
        if aligned:
            return token_blocks(tokens, plan, sizes, depth, after)
        return [
            jnp.concatenate(
                [
                    jnp.concatenate(
                        [
                            lax.dynamic_slice(
                                tokens,
                                (
                                    (tensor ^ j) * share + start,
                                    (chip ^ step) * depth + (core ^ i) * half,
                                ),
                                (min(size, share), half),
                            )
                            for i in range(CORES)
                        ],
                        axis=1,
                    )
                    for j in range(max(1, size // share))
                ]
            )
            for (step, start), size in zip(plan, sizes, strict=True)
        ]

    ahead = call(zero_kernel, shape((8, LANES), f32), flops=LONG)
    count, rows = windows[0].shape[0] - 2, windows[0].shape[1] * LANES // old_cols
    window, ends = call(
        first_weights_kernel,
        [shape((count + 2, rows, old_cols), bf16), shape((2, 2, rows, old_cols), bf16)],
        *windows,
        after=[ahead],
    )
    leaving_blocks = blocks_of(plan, sizes, [window])

    other = swap(window, "group", 1)
    arrived = [
        (step, swap(b, "dp", step * CORES))
        for (step, _), b in zip(plan, leaving_blocks, strict=True)
    ]

    mate_window = swap(window, "dp", 1)

    to_mate, to_next = call(
        border_kernel,
        [shape((4, rows, old_cols), bf16)] * 2,
        window,
        other,
        ends,
        after=[mate_window],
        flops=3 * 10**9,
    )
    inner, outer = swap(to_mate, "dp", 1), swap_border(to_next)

    turned = call(
        live_kernel, shape((slots, cols), bf16), counts, cotangent, scalars=1, after=[other]
    )
    blocks = [blocks_of([(0, 0)], [slots], [other])]
    for step in range(1, chips):
        block = [b for at, b in arrived if at == step]
        if step >= DIRECT:
            block += [swap(b, "tensor", j) for j in range(1, tensors) for b in list(block)]
        blocks.append(block)

    far, _ = lax.optimization_barrier((outer[:2], blocks[DIRECT]))

    mates = [mate_window] + [swap(w, "dp", 1) for w in (other, far)]
    weights = call(
        patch_weights_kernel,
        [shape((count, rows, cols), bf16)] * 2,
        old_offsets,
        window,
        other,
        *mates[:2],
        far,
        mates[2],
        scalars=1,
    )
    weights = [w.reshape(half, cols) for w in weights]

    steps = [chips - 1, *range(1, chips - 1)]
    parts = []
    for step in steps:
        parts.append(part(blocks[step], weights, bf16, after=parts[-1:]))
    back = [swap(p, "dp", step * CORES) for step, p in zip(steps, parts, strict=True)]

    leaving, staying = call(
        states_kernel,
        [shape((3, count // groups, rows, old_cols), dtype) for dtype in (bf16, f32)],
        old_offsets,
        *windows,
        inner,
        outer,
        scalars=1,
        after=parts[-1:],
    )
    incoming = swap(leaving, "group", 1)

    total = part(blocks[0], weights, f32, LONG)
    activated, delta = call(
        delta_kernel, [shape((slots, cols), bf16)] * 2, total, *back, turned
    )

    deltas = [delta] + [swap(delta, "dp", step * CORES) for step in steps]

    flat = [p for step in (0, *steps) for p in blocks[step]]
    gathered = call(
        gather_kernel,
        shape((chips * slots, depth), bf16),
        *flat,
        flops=LONG,
        after=[incoming, delta],
    )
    flops = 2 * half * cols * chips * slots
    tile = half // groups
    cuts = CUTS if tile % (CUTS * 16) == 0 and leaving.shape[1] % CUTS == 0 else 1
    first, second = call(
        mate_gradient_kernel, [shape((tile, cols), bf16)] * 2, gathered, *deltas, flops=flops
    )
    first = swap(first, "dp", 1)
    mine = call(own_gradient_kernel, shape((groups, tile, cols), f32), gathered, *deltas, flops=flops)
    second = swap(second, "dp", 1)
    sends = call(send_kernel, [shape((tile // cuts, cols), bf16)] * cuts, mine, first)
    new = []
    for cut, send in enumerate(sends):
        new = second_adam(cut, staying, incoming, mine, second, swap(send, "group", 1), new)
    activated = call(natural_kernel, shape((slots, cols), bf16), activated)
    return (activated, *new)


def solution(mesh):
    rows = P(("dp", "group"), "tensor")
    window = P(("tensor", "group"), "dp", None)
    return jax.shard_map(
        local,
        mesh=mesh,
        in_specs=(P(("dp", "group"), None), rows, P(), P(), window, window, window, window),
        out_specs=(rows, rows, rows, rows),
        check_vma=False,
    )
```

```python
import functools

import jax
import jax.numpy as jnp
from jax import lax
from jax.experimental import pallas as pl
from jax.experimental.pallas import tpu as pltpu
from jax.sharding import PartitionSpec as P

beta_one = 0.9
beta_two = 0.95
epsilon = 1e-08
learn_rate = 0.001
weight_decay = 0.1
first_step = 3.0
second_step = 4.0

LANES = 128
CORES = 2
f32, bf16 = jnp.float32, jnp.bfloat16
VMEM = 16 * 2**20
CUTS = 4
LAST = 1
DIRECT = 1
LONG = 10**11


def swap(value, axis, bits):
    pairs = [(source, source ^ bits) for source in range(lax.axis_size(axis))]
    return lax.ppermute(value, axis, pairs)


def swap_border(value):
    pairs = []
    for right in range(CORES, lax.axis_size("dp"), CORES):
        pairs += [(right - 1, right), (right, right - 1)]
    return lax.ppermute(value, "dp", pairs)


def adam_update(master, moment, variance, gradient, step_count):
    moment = beta_one * moment + (1.0 - beta_one) * gradient
    variance = beta_two * variance + (1.0 - beta_two) * gradient * gradient
    fix_one = 1.0 / (1.0 - beta_one**step_count)
    fix_two = 1.0 / (1.0 - beta_two**step_count)
    update = moment * fix_one / (jnp.sqrt(variance * fix_two) + epsilon) + weight_decay * master
    return (master - learn_rate * update, moment, variance)


def call(kernel, shapes, *args, scalars=0, flops=0, after=()):
    whole = pl.BlockSpec(memory_space=pltpu.VMEM)
    small = pl.BlockSpec(memory_space=pltpu.SMEM)
    touched = sum(a.size * a.dtype.itemsize for a in args)
    end = len(args)

    def body(*refs):
        kernel(*refs[:end], *refs[end + len(after) :])

    return pl.pallas_call(
        body,
        out_shape=shapes,
        in_specs=[small] * scalars
        + [whole] * (end - scalars)
        + [pl.BlockSpec(memory_space=pl.ANY)] * len(after),
        out_specs=jax.tree.map(lambda _: whole, shapes),
        compiler_params=pltpu.CompilerParams(vmem_limit_bytes=VMEM),
        cost_estimate=pl.CostEstimate(flops=flops, bytes_accessed=touched, transcendentals=0),
    )(*args, *after)


def shape(dims, dtype):
    return jax.ShapeDtypeStruct(dims, dtype)


def blocks_kernel(plan, skip, tokens, *refs):
    outs, sems = refs[skip:-1], refs[-1]
    rank, tensor = lax.axis_index("dp"), lax.axis_index("tensor")
    chip, core = rank // CORES, rank % CORES
    share = tokens.shape[0] // lax.axis_size("tensor")
    copies = []
    for (step, start), out in zip(plan, outs, strict=True):
        depth = out.shape[1] // CORES
        size = min(out.shape[0], share)
        for j in range(out.shape[0] // size):
            row = pl.multiple_of((tensor ^ j) * share + start, size)
            for i in range(CORES):
                col = pl.multiple_of(((chip ^ step) * CORES + (core ^ i)) * depth, depth)
                copies.append(
                    pltpu.make_async_copy(
                        tokens.at[pl.ds(row, size), pl.ds(col, depth)],
                        out.at[pl.ds(j * size, size), pl.ds(i * depth, depth)],
                        sems.at[len(copies)],
                    )
                )
    for copy in copies:
        copy.start()
    for copy in copies:
        copy.wait()


def token_blocks(tokens, plan, sizes, depth, after):
    outs = [shape((size, depth), bf16) for size in sizes]
    share = tokens.shape[0] // lax.axis_size("tensor")
    copies = sum(CORES * max(1, size // share) for size in sizes)
    return pl.pallas_call(
        functools.partial(blocks_kernel, plan, len(after)),
        out_shape=outs,
        in_specs=[pl.BlockSpec(memory_space=pl.ANY)] * (1 + len(after)),
        out_specs=[pl.BlockSpec(memory_space=pltpu.VMEM)] * len(outs),
        scratch_shapes=[pltpu.SemaphoreType.DMA((copies,))],
        compiler_params=pltpu.CompilerParams(vmem_limit_bytes=VMEM),
        cost_estimate=pl.CostEstimate(flops=0, bytes_accessed=10**6, transcendentals=0),
    )(tokens, *after)


def updated(windows, block, h, rows, per):
    picks = pl.ds(h, rows, stride=per) if per > 1 else pl.ds(0, rows)
    return adam_update(*[w[block, picks, :] for w in windows], first_step)


def first_weights_kernel(*refs):
    windows, out, ends = refs[:4], refs[4], refs[5]
    blocks, rows, cols = out.shape
    per = cols // LANES
    for k in range(blocks):
        for h in range(per):
            at = slice(h * LANES, (h + 1) * LANES)
            values = updated(windows, k, h, rows, per)
            out[k, :, at] = values[0].astype(bf16)
            if k in (0, blocks - 1):
                for i in range(2):
                    ends[min(k, 1), i, :, at] = values[i + 1].astype(bf16)


def border_kernel(window, other, ends, to_mate, to_next):
    first = lax.axis_index("dp") % CORES == 0
    last = window.shape[0] - 1
    pairs = [(window[0], window[last]), (other[0], other[last])]
    pairs += [(ends[0, i], ends[1, i]) for i in range(2)]
    for i, (head, tail) in enumerate(pairs):
        head, tail = head.astype(f32), tail.astype(f32)
        to_mate[i] = jnp.where(first, tail, head).astype(bf16)
        to_next[i] = jnp.where(first, head, tail).astype(bf16)


def live_bounds(offsets, span, rank, other):
    slab = lax.axis_index("tensor") * lax.axis_size("group") + (lax.axis_index("group") ^ other)
    start = rank * span
    return offsets[slab, rank] - start, offsets[slab, rank + 1] - start


def place_of(rows, cols, first):
    place = lax.broadcasted_iota(jnp.int32, (rows, cols), 0) * cols
    return first + place + lax.broadcasted_iota(jnp.int32, (rows, cols), 1)


def patch_weights_kernel(offsets, own, other, mate_own, mate_other, outer, mate_outer, mine, mate):
    rows, cols = own.shape[1:]
    count = own.shape[0] - 2
    span = count * rows * cols
    rank = lax.axis_index("dp")
    first = rank % CORES == 0
    for i, (here, there) in enumerate(((own, mate_own), (other, mate_other))):
        at = slice(i * cols, (i + 1) * cols)
        for out, window, near, far, swapped in (
            (mine, here, there, outer, 0),
            (mate, there, here, mate_outer, 1),
        ):
            low, high = live_bounds(offsets, span, rank ^ swapped, i)
            left_far = first if swapped == 0 else jnp.logical_not(first)
            before = place_of(rows, cols, 0) < low
            after = place_of(rows, cols, span - rows * cols) >= high
            far_end = far[i].astype(f32)
            left = jnp.where(left_far, far_end, near[count + 1].astype(f32))
            right = jnp.where(left_far, near[0].astype(f32), far_end)
            out[0, :, at] = jnp.where(before, left, window[1].astype(f32)).astype(bf16)
            out[1 : count - 1, :, at] = window[2:count]
            out[count - 1, :, at] = jnp.where(after, right, window[count].astype(f32)).astype(bf16)


def states_kernel(offsets, *refs):
    windows, (inner, outer), outs = refs[:4], refs[4:6], refs[6:]
    _, half, rows, cols = outs[0].shape
    per = cols // LANES
    span = 2 * half * rows * cols
    low, high = live_bounds(offsets, span, lax.axis_index("dp"), 0)
    first = lax.axis_index("dp") % CORES == 0
    group = lax.axis_index("group")
    for tile, out in zip((1 - group, group), outs, strict=True):
        for k in range(half):
            block = tile * half + k
            for h in range(per):
                at = slice(h * LANES, (h + 1) * LANES)
                values = updated(windows, block + 1, h, rows, per)
                place = lax.broadcasted_iota(jnp.int32, (rows, LANES), 0) * cols
                place = place + lax.broadcasted_iota(jnp.int32, (rows, LANES), 1)
                place = place + (block * rows * cols + h * LANES)
                for i in range(3):
                    value = values[i]
                    at_end = (0, 2, 3)[i]
                    near = inner[at_end, :, at].astype(f32)
                    far = outer[at_end, :, at].astype(f32)
                    if k == 0:
                        value = jnp.where(place < low, jnp.where(first, far, near), value)
                    if k == half - 1:
                        value = jnp.where(place >= high, jnp.where(first, near, far), value)
                    out[i, k, :, at] = value.astype(out.dtype)


def part_kernel(pieces, *refs):
    mine, mate, out = refs[pieces:]
    rows = jnp.concatenate([r[...] for r in refs[:pieces]], axis=0)
    depth = mine.shape[0]
    value = jnp.dot(rows[:, :depth], mine[...], preferred_element_type=f32)
    value = value + jnp.dot(rows[:, depth:], mate[...], preferred_element_type=f32)
    out[...] = value.astype(out.dtype)


def part(pieces, weights, dtype, flops=0, after=()):
    rows = sum(p.shape[0] for p in pieces)
    cols = weights[0].shape[1]
    return call(
        functools.partial(part_kernel, len(pieces)),
        shape((rows, cols), dtype),
        *pieces,
        *weights,
        flops=flops or 2 * rows * pieces[0].shape[1] * cols,
        after=after,
    )


def own_order(rows, cols):
    tensors, groups = lax.axis_size("tensor"), lax.axis_size("group")
    share, wide = rows // tensors, cols // groups
    for j in range(tensors):
        row = pl.multiple_of((lax.axis_index("tensor") ^ j) * share, share)
        for i in range(groups):
            col = pl.multiple_of((lax.axis_index("group") ^ i) * wide, wide)
            here = (slice(j * share, (j + 1) * share), slice(i * wide, (i + 1) * wide))
            yield here, (pl.ds(row, share), pl.ds(col, wide)), row


def live_kernel(counts, cotangent, out):
    live = counts[lax.axis_index("dp") * lax.axis_size("group") + lax.axis_index("group")]
    for here, there, first_row in own_order(*cotangent.shape):
        value = cotangent[there].astype(f32)
        row = first_row + lax.broadcasted_iota(jnp.int32, value.shape, 0)
        out[here] = jnp.where(row < live, value, 0.0).astype(bf16)


def delta_kernel(*refs):
    own, (cotangent, activated, delta) = refs[0], refs[-3:]
    preact = own[...]
    for r in refs[1:-3]:
        preact = preact + r[...].astype(f32)
    sigmoid = 1.0 / (1.0 + jnp.exp(-preact))
    activated[...] = (preact * sigmoid).astype(bf16)
    derivative = sigmoid * (1.0 + preact * (1.0 - sigmoid))
    delta[...] = (cotangent[...].astype(f32) * derivative).astype(bf16)


def natural_kernel(value, out):
    for here, there, _ in own_order(*value.shape):
        out[there] = value[here]


def zero_kernel(out):
    out[...] = jnp.zeros(out.shape, out.dtype)


def gather_kernel(*refs):
    start = 0
    for r in refs[:-1]:
        refs[-1][start : start + r.shape[0]] = r[...]
        start += r.shape[0]


def mate_gradient_kernel(tokens, *refs):
    deltas, (first, second) = refs[:-2], refs[-2:]
    depth = tokens.shape[1] // CORES
    value = lax.dot_general(
        tokens[:, depth:],
        jnp.concatenate([r[...] for r in deltas], axis=0),
        (((0,), (0,)), ((), ())),
        preferred_element_type=f32,
    )
    tile = first.shape[0]
    low = lax.axis_index("group") == 0
    first[...] = jnp.where(low, value[tile:], value[:tile]).astype(bf16)
    second[...] = jnp.where(low, value[:tile], value[tile:]).astype(bf16)


def own_gradient_kernel(tokens, *refs):
    deltas, out = refs[:-1], refs[-1]
    depth = tokens.shape[1] // CORES
    value = lax.dot_general(
        tokens[:, :depth],
        jnp.concatenate([r[...] for r in deltas], axis=0),
        (((0,), (0,)), ((), ())),
        preferred_element_type=f32,
    )
    tile = out.shape[1]
    for i in range(out.shape[0]):
        out[i] = value[i * tile : (i + 1) * tile]


def send_kernel(mine, received, *outs):
    other = 1 - lax.axis_index("group")
    cols = received.shape[1] // 2
    rows = outs[0].shape[0]
    for i, out in enumerate(outs):
        at = slice(i * rows, (i + 1) * rows)
        value = (mine[other, at] + received[at].astype(f32)).astype(bf16)
        out[:, :cols] = value[:, cols:]
        out[:, cols:] = value[:, :cols]


def second_adam_kernel(cut, staying, incoming, mine, received, back, *refs):
    outs, results, sems = refs[-7:-4], refs[-4:-1], refs[-1]
    _, half, rows, cols = staying.shape
    group = lax.axis_index("group")
    size = back.shape[0] // rows
    for k in range(size):
        block = cut * size + k
        for i, states in enumerate((staying, incoming)):
            at = slice(i * cols, (i + 1) * cols)
            there = pl.ds(pl.multiple_of((group ^ i) * cols, cols), cols)
            tile_rows = slice(block * rows, (block + 1) * rows)
            here = slice(k * rows, (k + 1) * rows)
            gradient = mine[group, tile_rows, at] + received[tile_rows, at].astype(f32)
            gradient = gradient + back[here, at].astype(f32)
            values = [states[j, block].astype(f32) for j in range(3)]
            result = adam_update(*values, gradient, second_step)
            for ref, value in zip(results, result, strict=True):
                ref[here, there] = value
    total = back.shape[0]
    copies = [
        pltpu.make_async_copy(ref, out.at[pl.ds(cut * total, total)], sems.at[i])
        for i, (ref, out) in enumerate(zip(results, outs, strict=True))
    ]
    for copy in copies:
        copy.start()
    for copy in copies:
        copy.wait()


def second_adam(cut, staying, incoming, mine, received, back, done):
    rows, cols = received.shape
    whole = pl.BlockSpec(memory_space=pltpu.VMEM)
    anywhere = pl.BlockSpec(memory_space=pl.ANY)
    return pl.pallas_call(
        functools.partial(second_adam_kernel, cut),
        out_shape=[shape((rows, cols), f32)] * 3,
        in_specs=[whole] * 5 + [anywhere] * len(done),
        out_specs=[anywhere] * 3,
        scratch_shapes=[pltpu.VMEM(back.shape, f32)] * 3 + [pltpu.SemaphoreType.DMA((3,))],
        input_output_aliases={5 + i: i for i in range(len(done))},
        compiler_params=pltpu.CompilerParams(vmem_limit_bytes=VMEM),
        cost_estimate=pl.CostEstimate(flops=0, bytes_accessed=10**6, transcendentals=0),
    )(staying, incoming, mine, received, back, *done)


def local(tokens, cotangent, counts, old_offsets, old_master, old_moment, old_variance, old_grad):
    ranks = lax.axis_size("dp")
    chips = ranks // CORES
    groups = lax.axis_size("group")
    tensors = lax.axis_size("tensor")
    rank = lax.axis_index("dp")
    chip, core = rank // CORES, rank % CORES
    tensor = lax.axis_index("tensor")
    slots, width = tokens.shape
    cols = cotangent.shape[1]
    old_cols = cols // groups
    depth = width // chips
    half = depth // CORES
    share = slots // tensors

    length = old_master.shape[2]
    margin = length // 10
    windows = [
        w.reshape(10, margin // LANES, LANES)
        for w in (old_master, old_moment, old_variance, old_grad)
    ]
    aligned = half % LANES == 0 and share % 16 == 0
    last = share // LAST if aligned and share % (16 * LAST) == 0 else share
    plan = [(step, 0) for step in range(1, chips - 1)]
    plan += [(chips - 1, start) for start in range(0, share, last)]
    sizes = [slots if step < DIRECT else share for step in range(1, chips - 1)]
    sizes += [last] * (share // last)

    def blocks_of(plan, sizes, after):
        if aligned:
            return token_blocks(tokens, plan, sizes, depth, after)
        return [
            jnp.concatenate(
                [
                    jnp.concatenate(
                        [
                            lax.dynamic_slice(
                                tokens,
                                (
                                    (tensor ^ j) * share + start,
                                    (chip ^ step) * depth + (core ^ i) * half,
                                ),
                                (min(size, share), half),
                            )
                            for i in range(CORES)
                        ],
                        axis=1,
                    )
                    for j in range(max(1, size // share))
                ]
            )
            for (step, start), size in zip(plan, sizes, strict=True)
        ]

    ahead = call(zero_kernel, shape((8, LANES), f32), flops=LONG)
    count, rows = windows[0].shape[0] - 2, windows[0].shape[1] * LANES // old_cols
    window, ends = call(
        first_weights_kernel,
        [shape((count + 2, rows, old_cols), bf16), shape((2, 2, rows, old_cols), bf16)],
        *windows,
        after=[ahead],
    )
    leaving_blocks = blocks_of(plan, sizes, [window])

    other = swap(window, "group", 1)
    arrived = [
        (step, swap(b, "dp", step * CORES))
        for (step, _), b in zip(plan, leaving_blocks, strict=True)
    ]

    mate_window = swap(window, "dp", 1)

    to_mate, to_next = call(
        border_kernel,
        [shape((4, rows, old_cols), bf16)] * 2,
        window,
        other,
        ends,
        after=[mate_window],
        flops=3 * 10**9,
    )
    inner, outer = swap(to_mate, "dp", 1), swap_border(to_next)

    blocks = [blocks_of([(0, 0)], [slots], [other])]
    for step in range(1, chips):
        block = [b for at, b in arrived if at == step]
        if step >= DIRECT:
            block += [swap(b, "tensor", j) for j in range(1, tensors) for b in list(block)]
        blocks.append(block)

    far, _ = lax.optimization_barrier((outer[:2], blocks[DIRECT]))

    mates = [mate_window] + [swap(w, "dp", 1) for w in (other, far)]
    weights = call(
        patch_weights_kernel,
        [shape((count, rows, cols), bf16)] * 2,
        old_offsets,
        window,
        other,
        *mates[:2],
        far,
        mates[2],
        scalars=1,
    )
    weights = [w.reshape(half, cols) for w in weights]

    steps = [chips - 1, *range(1, chips - 1)]
    parts = []
    for step in steps:
        parts.append(part(blocks[step], weights, bf16, after=parts[-1:]))
    back = [swap(p, "dp", step * CORES) for step, p in zip(steps, parts, strict=True)]

    turned = call(
        live_kernel, shape((slots, cols), bf16), counts, cotangent, scalars=1, after=parts[-1:]
    )

    leaving, staying = call(
        states_kernel,
        [shape((3, count // groups, rows, old_cols), dtype) for dtype in (bf16, f32)],
        old_offsets,
        *windows,
        inner,
        outer,
        scalars=1,
        after=parts[-1:],
    )
    incoming = swap(leaving, "group", 1)

    total = part(blocks[0], weights, f32, LONG)
    activated, delta = call(
        delta_kernel, [shape((slots, cols), bf16)] * 2, total, *back, turned
    )

    deltas = [delta] + [swap(delta, "dp", step * CORES) for step in steps]

    flat = [p for step in (0, *steps) for p in blocks[step]]
    gathered = call(
        gather_kernel,
        shape((chips * slots, depth), bf16),
        *flat,
        flops=LONG,
        after=[incoming, delta],
    )
    flops = 2 * half * cols * chips * slots
    tile = half // groups
    cuts = CUTS if tile % (CUTS * 16) == 0 and leaving.shape[1] % CUTS == 0 else 1
    first, second = call(
        mate_gradient_kernel, [shape((tile, cols), bf16)] * 2, gathered, *deltas, flops=flops
    )
    first = swap(first, "dp", 1)
    mine = call(own_gradient_kernel, shape((groups, tile, cols), f32), gathered, *deltas, flops=flops)
    second = swap(second, "dp", 1)
    sends = call(send_kernel, [shape((tile // cuts, cols), bf16)] * cuts, mine, first)
    new = []
    for cut, send in enumerate(sends):
        new = second_adam(cut, staying, incoming, mine, second, swap(send, "group", 1), new)
    activated = call(natural_kernel, shape((slots, cols), bf16), activated)
    return (activated, *new)


def solution(mesh):
    rows = P(("dp", "group"), "tensor")
    window = P(("tensor", "group"), "dp", None)
    return jax.shard_map(
        local,
        mesh=mesh,
        in_specs=(P(("dp", "group"), None), rows, P(), P(), window, window, window, window),
        out_specs=(rows, rows, rows, rows),
        check_vma=False,
    )
```
